256 devices in a mesh: rows: 16 (over z, core), group: 16 (over x, y).
Axes of the slice: x: 4, y: 4, z: 8, core: 2. Of those that a mesh axis runs over, the one named last changes fastest.
Arguments:
- embeddings: bfloat16 [65536, 256], P(('rows', 'group')), may hold values from -6 to 6
- fine_labels: int32 [65536], P(('rows', 'group')), may hold values from 0 to 16383
- prototypes: bfloat16 [16384, 256], P('group'), may hold values from -2.25 to 2.25
- coarse_protos: bfloat16 [1024, 256], replicated, may hold values from -0.190625 to 0.190625
- coarse_labels: int32 [16384], P('group'), may hold values from 0 to 1023
Outputs:
- grad_embeddings: float32 [65536, 256], P(('rows', 'group'))
- grad_prototypes: float32 [16384, 256], P('group')
- new_prototypes: float32 [16384, 256], P('group')
- grad_coarse: float32 [1024, 256], replicated
- total_loss: float32 [], replicated
The draws below stay inside these ranges and needn't reach their ends.
All inputs are finite; a program needn't handle non-finite values.
Results may differ from the reference program's by a relative error of at most 0.007.
Values may be sent and summed in bfloat16 or wider, within the bound.
A program may use at most 64 MiB of HBM per device.

```python
import math
import jax
import jax.numpy as jnp
import numpy as np
from jax import lax

D = 256
K = 16384
KC = 1024
N = 65536


def draw_embeddings(key, part):
    key = jax.random.fold_in(key, 1)
    values = jnp.clip(jax.random.normal(key, (N, D), jnp.float32), -6.0, 6.0)
    return values.astype(jnp.bfloat16)


def draw_prototypes(key, part):
    key = jax.random.fold_in(key, 2)
    scale = 4.0 / math.sqrt(D)
    values = jnp.clip(scale * jax.random.normal(key, (K, D), jnp.float32), -6.0 * scale, 6.0 * scale)
    return values.astype(jnp.bfloat16)


def draw_coarse_protos(key, part):
    key = jax.random.fold_in(key, 3)
    scale = 1.0 / math.sqrt(D)
    values = jnp.clip(scale * jax.random.normal(key, (KC, D), jnp.float32), -3.0 * scale, 3.0 * scale)
    return values.astype(jnp.bfloat16)


def place_ends(drawn, stream_key, smallest, top_value):
    place = [jax.random.randint(jax.random.fold_in(stream_key, axis), (), 0, length) for axis, length in enumerate(drawn.shape)]
    longest = drawn.shape.index(max(drawn.shape))
    neighbour = place[:longest] + [(place[longest] + 1) % drawn.shape[longest]] + place[longest + 1:]
    return drawn.at[tuple(place)].set(smallest).at[tuple(neighbour)].set(top_value)


def rank_table(count, slope):
    portions = [(1 << 20) // math.isqrt(standing ** slope) + 1 for standing in range(1, count + 1)]
    width = 1 + sum(portions) // (1 << 30)
    return np.cumsum(np.array([max(1, weight // width) for weight in portions]))


def ranked(rng, dims, amount, lean):
    table = rank_table(amount, lean)
    ticket = jax.random.randint(jax.random.fold_in(rng, 1), dims, 0, int(table[amount - 1]))
    grade = jnp.searchsorted(jnp.asarray(table, jnp.int32), ticket, side="right")
    return jax.random.permutation(jax.random.fold_in(rng, 2), amount)[grade].astype(jnp.int32)


def setup_inputs(seed: int = 0) -> dict:
    splits = jax.random.split(jax.random.key(seed), 6)
    return {
        "embeddings": draw_embeddings(jax.random.fold_in(splits[5], 71), 0),
        "fine_labels": place_ends(ranked(splits[1], (N,), K, 1), jax.random.fold_in(splits[1], 3), 0, K - 1).astype(jnp.int32),
        "prototypes": draw_prototypes(jax.random.fold_in(splits[5], 71), 0),
        "coarse_protos": draw_coarse_protos(jax.random.fold_in(splits[5], 71), 0),
        "coarse_labels": place_ends(ranked(splits[4], (K,), KC, 1), jax.random.fold_in(splits[4], 3), 0, KC - 1).astype(jnp.int32),
    }


def reference(embeddings, fine_labels, prototypes, coarse_protos, coarse_labels):
    emb_float = embeddings.astype(jnp.float32)
    inverse = lax.rsqrt(lax.optimization_barrier(jnp.sum(emb_float * emb_float, axis=1, keepdims=True)) + 1e-06)
    unit = emb_float * inverse
    unit_half = unit.astype(jnp.bfloat16)
    block_rows = min(1024, N)
    nblock = N // block_rows
    columns = jnp.arange(K, dtype=jnp.int32)

    def grads_block(running, inputs):
        grad_proto, fine_sum = running
        rows_half, labels = inputs
        logits = 10.0 * lax.dot_general(rows_half, prototypes, (((1,), (1,)), ((), ())), preferred_element_type=jnp.float32)
        largest = lax.optimization_barrier(jnp.max(logits, axis=1))
        log_total = largest + jnp.log(lax.optimization_barrier(jnp.sum(jnp.exp(logits - largest[:, None]), axis=1)))
        member = columns[None, :] == labels[:, None]
        target = lax.optimization_barrier(jnp.sum(jnp.where(member, logits, jnp.float32(0.0)), axis=1))
        delta = (10.0 * (jnp.exp(logits - log_total[:, None]) - member.astype(jnp.float32))).astype(jnp.bfloat16)
        row_terms = jnp.dot(delta, prototypes, preferred_element_type=jnp.float32)
        grad_proto = grad_proto + lax.dot_general(delta, rows_half, (((0,), (0,)), ((), ())), preferred_element_type=jnp.float32)
        return ((grad_proto, fine_sum + jnp.sum(log_total - target)), row_terms)
    start_sums = (jnp.zeros((K, D), jnp.float32), jnp.zeros((), jnp.float32))
    (proto_fine, fine_loss), row_terms = lax.scan(grads_block, start_sums, (unit_half.reshape(nblock, block_rows, D), fine_labels.reshape(nblock, block_rows)))
    row_grad = row_terms.reshape(N, D)
    grad_embeddings = inverse * (row_grad - unit * lax.optimization_barrier(jnp.sum(unit * row_grad, axis=1, keepdims=True)))
    member_sum = jax.ops.segment_sum(unit_half.astype(jnp.float32), fine_labels, K)
    coarse_logits = 10.0 * lax.dot_general(prototypes, coarse_protos, (((1,), (1,)), ((), ())), preferred_element_type=jnp.float32)
    largest = lax.optimization_barrier(jnp.max(coarse_logits, axis=1))
    coarse_total = largest + jnp.log(lax.optimization_barrier(jnp.sum(jnp.exp(coarse_logits - largest[:, None]), axis=1)))
    member = jnp.arange(KC, dtype=jnp.int32)[None, :] == coarse_labels[:, None]
    target = lax.optimization_barrier(jnp.sum(jnp.where(member, coarse_logits, jnp.float32(0.0)), axis=1))
    coarse_loss = jnp.sum(coarse_total - target)
    coarse_delta = (10.0 * (jnp.exp(coarse_logits - coarse_total[:, None]) - member.astype(jnp.float32))).astype(jnp.bfloat16)
    grad_prototypes = K / N * proto_fine + jnp.dot(coarse_delta, coarse_protos, preferred_element_type=jnp.float32)
    grad_coarse = KC / K * lax.dot_general(coarse_delta, prototypes, (((0,), (0,)), ((), ())), preferred_element_type=jnp.float32)
    proto_float = prototypes.astype(jnp.float32)
    proto_norm = jnp.sqrt(lax.optimization_barrier(jnp.sum(proto_float * proto_float, axis=1, keepdims=True)) + 1e-06)
    direction = member_sum * lax.rsqrt(lax.optimization_barrier(jnp.sum(member_sum * member_sum, axis=1, keepdims=True)) + 1e-06)
    new_prototypes = 0.5 * proto_float + 0.5 * proto_norm * direction
    total_loss = fine_loss / N + coarse_loss / K
    return (grad_embeddings, grad_prototypes, new_prototypes, grad_coarse, total_loss)
```

```python
import functools

import jax
import jax.numpy as jnp
from jax import lax
from jax.experimental import pallas as pl
from jax.experimental.pallas import tpu as pltpu
from jax.sharding import PartitionSpec as P

MESH = pl.DeviceIdType.MESH
F32 = jnp.float32
BF16 = jnp.bfloat16
ROWS = 256
D = 256
KL = 1024
KC = 1024
G = 16
NCH = KL // 256
N_GATHER = 40
NT = (((1,), (1,)), ((), ()))


def dot(a, b):
    return jnp.dot(a, b, preferred_element_type=F32)


def dot_nt(a, b):
    return lax.dot_general(a, b, NT, preferred_element_type=F32)


def column_sum(value):
    return jnp.sum(value, axis=0, keepdims=True)


def total(value):
    return jnp.sum(jnp.sum(value, axis=0, keepdims=True), axis=1, keepdims=True)


def kernel(
    emb, lab, protos, coarse, clab,
    o_emb, o_pg, o_new, o_cg, o_loss,
    gbuf, labs, unit_s, inv_s, protos_t, coarse_t, lscr, ohs, ebuf, obuf, lbuf, us, rout, rin, own_rt,
    mem, soft, cg, cpart_t, cpart, stats, mmax, wbuf,
    cg_out, cg_in, cg_all, cg_fin, core_in, z_out, z_in, fin, loss_core, loss_z,
    gs, gr, labs_s, labs_r, cgo_s, cgo_r, cga_s, cga_r, cgz_s, cgz_r, st_s, st_r, rw_s, rw_r,
    co_s, co_r, zo_s, zo_r, za_s, za_r, ca_s, ca_r, ls_s, ls_r,
):
    r = lax.axis_index("rows")
    g = lax.axis_index("group")
    z, c = r // 2, lax.rem(r, 2)
    x, y = g // 4, lax.rem(g, 4)
    other = r + 1 - 2 * c

    def blk(dx, dy):
        return lax.rem(x + dx, 4) * 4 + lax.rem(y + dy, 4)

    def plane(d):
        return (r, lax.rem(g + d, G))

    def column(d):
        return (lax.rem(r + 2 * d, 16), g)

    def zof(d):
        return lax.rem(z + d, 8)

    barrier = pltpu.get_barrier_semaphore()
    for d in range(1, G):
        pl.semaphore_signal(barrier, inc=1, device_id=plane(d), device_id_type=MESH)
    for d in range(1, 8):
        pl.semaphore_signal(barrier, inc=1, device_id=column(d), device_id_type=MESH)
    pl.semaphore_signal(barrier, inc=1, device_id=(other, g), device_id_type=MESH)

    e32 = emb[...].astype(F32)
    inv = lax.rsqrt(jnp.sum(e32 * e32, axis=1, keepdims=True) + 1e-06)
    unit = e32 * inv
    unit_s[...] = unit
    inv_s[...] = jnp.broadcast_to(inv, (ROWS, 128))
    gbuf[g] = unit.astype(BF16)
    labs[g] = lab[...]

    for i in range(NCH):
        protos_t[:, i * 256 : (i + 1) * 256] = protos[i * 256 : (i + 1) * 256, :].astype(F32).T.astype(BF16)
        coarse_t[:, i * 256 : (i + 1) * 256] = coarse[i * 256 : (i + 1) * 256, :].astype(F32).T.astype(BF16)

    iota = lax.broadcasted_iota(jnp.int32, (256, 256), 0)
    cg[...] = jnp.zeros_like(cg)
    mem[...] = jnp.zeros_like(mem)

    def coarse_step(kb, closs):
        cols = pl.ds(pl.multiple_of(kb * 256, 256), 256)
        u = protos[cols, :]
        peak = jnp.full((1, 256), -jnp.inf, F32)
        for i in range(NCH):
            logits = 10.0 * dot_nt(coarse[i * 256 : (i + 1) * 256, :], u)
            lscr[i * 256 : (i + 1) * 256, :] = logits
            peak = jnp.maximum(peak, jnp.max(logits, axis=0, keepdims=True))
        expsum = jnp.zeros((1, 256), F32)
        target = jnp.zeros((1, 256), F32)
        labels = clab[pl.ds(kb, 1), :]
        for i in range(NCH):
            logits = lscr[i * 256 : (i + 1) * 256, :]
            target = target + column_sum(jnp.where(iota == labels - i * 256, logits, 0.0))
            e = jnp.exp(logits - peak)
            expsum = expsum + column_sum(e)
            lscr[i * 256 : (i + 1) * 256, :] = e
        share = 1.0 / expsum
        for i in range(NCH):
            member = (iota == labels - i * 256).astype(F32)
            ohs[i * 256 : (i + 1) * 256, :] = (10.0 * (lscr[i * 256 : (i + 1) * 256, :] * share - member)).astype(BF16)
        cpart_t[:, cols] = dot(coarse_t[...], ohs[...])
        for i in range(NCH):
            cg[i * 256 : (i + 1) * 256, :] += dot(ohs[i * 256 : (i + 1) * 256, :], u)
        return closs + total(peak + jnp.log(expsum) - target)

    coarse_loss = lax.fori_loop(0, NCH, coarse_step, jnp.zeros((1, 1), F32))

    pl.semaphore_wait(barrier, 23)

    A, B = (0, 128), (128, 128)
    A0, A1, B0, B1 = (0, 64), (64, 64), (128, 64), (192, 64)
    count = [0]

    def send(block, rows, dx, dy):
        k = count[0]
        count[0] += 1
        piece = gbuf.at[block, pl.ds(*rows)]
        cp = pltpu.make_async_remote_copy(
            piece, piece, gs.at[k], gr.at[k], device_id=(r, blk(dx, dy)), device_id_type=MESH
        )
        cp.start()
        return cp

    def both_y(block):
        return send(block, A, 0, 1), send(block, A, 0, 3)

    def both_x(block):
        return send(block, B, 1, 0), send(block, B, 3, 0)

    sends, tails = [], []

    def on_y(cp, dx, up):
        cp.wait_recv()
        out = send(blk(dx, 3 if up else 1), A0 if up else A1, 0, 1 if up else 3)
        tails.append(out)
        return out

    def on_x(cp, dy, up):
        cp.wait_recv()
        out = send(blk(3 if up else 1, dy), B0 if up else B1, 1 if up else 3, 0)
        tails.append(out)
        return out

    a1, a2 = send(g, A, 1, 0), send(g, A, 3, 0)
    b1, b2 = send(g, B, 0, 1), send(g, B, 0, 3)
    a3, a4 = both_y(g)
    b3, b4 = both_x(g)

    def lab_copy(d):
        return pltpu.make_async_remote_copy(
            labs.at[g], labs.at[g], labs_s.at[d], labs_r.at[d], device_id=plane(d), device_id_type=MESH
        )

    def lab_arrival(d):
        slot = labs.at[lax.rem(g + G - d, G)]
        return pltpu.make_async_remote_copy(
            slot, slot, labs_s.at[d], labs_r.at[d], device_id=plane(d), device_id_type=MESH
        )

    @pl.loop(1, G)
    def _(d):
        lab_copy(d).start()

    base = c * 512 + z * 64
    for q in range(G):
        cg_out[q] = cg[pl.ds(pl.multiple_of(base + 8 * (q // 2), 8), 8), (q % 2) * 128 : (q % 2) * 128 + 128]

    def cgo_copy(d):
        return pltpu.make_async_remote_copy(
            cg_out.at[lax.rem(g + d, G)], cg_in.at[d], cgo_s.at[d], cgo_r.at[d], device_id=plane(d), device_id_type=MESH
        )

    @pl.loop(1, G)
    def _(d):
        cgo_copy(d).start()

    def first_pass(i):
        u = gbuf[i]
        peak = jnp.full((1, 256), -jnp.inf, F32)
        for j in range(NCH):
            logits = dot_nt(protos[j * 256 : (j + 1) * 256, :], u)
            lscr[j * 256 : (j + 1) * 256, :] = logits
            peak = jnp.maximum(peak, jnp.max(logits, axis=0, keepdims=True))
        expsum = jnp.zeros((1, 256), F32)
        labels = labs[i] - g * KL
        for j in range(NCH):
            rows = slice(j * 256, (j + 1) * 256)
            e = jnp.exp(10.0 * (lscr[rows, :] - peak))
            expsum = expsum + column_sum(e)
            ebuf[i, rows, :] = e.astype(BF16)
            member = (iota == labels - j * 256).astype(F32).astype(BF16)
            ohs[rows, :] = member
            mem[rows, :] += dot(member, u)
        obuf[i] = dot(protos_t[...], ebuf[i])
        lbuf[i] = dot(protos_t[...], ohs[...]).astype(BF16)
        mmax[pl.ds(i, 1), :] = 10.0 * peak
        stats[g, pl.ds(i, 1), :] = 10.0 * peak + jnp.log(expsum)

    first_pass(g)

    a1.wait_recv()
    f1 = send(blk(3, 0), A0, 1, 0)
    p1, p2 = both_y(blk(3, 0))
    b1.wait_recv()
    g1 = send(blk(0, 3), B0, 0, 1)
    q1, q2 = both_x(blk(0, 3))
    a2.wait_recv()
    f2 = send(blk(1, 0), A1, 3, 0)
    p3, p4 = both_y(blk(1, 0))
    b2.wait_recv()
    g2 = send(blk(0, 1), B1, 0, 3)
    q3, q4 = both_x(blk(0, 1))
    sends += [a1, a2, b1, b2, a3, a4, b3, b4, f1, f2, g1, g2, p1, p2, p3, p4, q1, q2, q3, q4]
    a3f, b3f, a4f, b4f = on_y(a3, 0, True), on_x(b3, 0, True), on_y(a4, 0, False), on_x(b4, 0, False)

    @pl.loop(1, G)
    def _(d):
        lab_arrival(d).wait_recv()

    @pl.loop(0, 4)
    def _(k):
        far = 1 + 2 * lax.rem(k, 2)
        first_pass(blk((1 - k // 2) * far, (k // 2) * far))

    f1.wait_recv()
    f2.wait_recv()
    p5, p6 = both_y(blk(2, 0))
    g1.wait_recv()
    g2.wait_recv()
    q5, q6 = both_x(blk(0, 2))
    sends += [p5, p6, q5, q6]
    p1f, q1f, p2f, q2f = on_y(p1, 3, True), on_x(q1, 3, True), on_y(p2, 3, False), on_x(q2, 3, False)
    p3f, q3f, p4f, q4f = on_y(p3, 1, True), on_x(q3, 1, True), on_y(p4, 1, False), on_x(q4, 1, False)
    for cp in (a3f, b3f, a4f, b4f):
        cp.wait_recv()

    @pl.loop(0, 4)
    def _(k):
        first_pass(blk(1 + 2 * (k // 2), 1 + 2 * lax.rem(k, 2)))

    p5f, q5f, p6f, q6f = on_y(p5, 2, True), on_x(q5, 2, True), on_y(p6, 2, False), on_x(q6, 2, False)

    @pl.loop(1, G)
    def _(d):
        cgo_copy(d).wait_recv()

    tile = cg_out[g]
    for d in range(1, G):
        tile = tile + cg_in[d]
    cg_all[g] = (KC / (KL * G)) * tile

    def cga_copy(d):
        return pltpu.make_async_remote_copy(
            cg_all.at[g], cg_all.at[g], cga_s.at[d], cga_r.at[d], device_id=plane(d), device_id_type=MESH
        )

    def cga_arrival(d):
        slot = cg_all.at[lax.rem(g + G - d, G)]
        return pltpu.make_async_remote_copy(
            slot, slot, cga_s.at[d], cga_r.at[d], device_id=plane(d), device_id_type=MESH
        )

    @pl.loop(1, G)
    def _(d):
        cga_copy(d).start()

    for cp in (p1f, q1f, p2f, q2f, p3f, q3f, p4f, q4f):
        cp.wait_recv()

    @pl.loop(0, 6)
    def _(k):
        late = lax.min(k // 2, 1)
        m = k - 2
        even = 1 + 2 * lax.rem(k, 2)
        lines = k // 4
        dx0, dy0 = 2 - 2 * k, 2 * k
        dx1 = 2 * (1 - lines) + even * lines
        dy1 = even * (1 - lines) + 2 * lines
        first_pass(blk((1 - late) * dx0 + late * dx1, (1 - late) * dy0 + late * dy1))

    @pl.loop(1, G)
    def _(d):
        cga_arrival(d).wait_recv()

    for q in range(G):
        cg_fin[c, z, (q // 2) * 8 : (q // 2) * 8 + 8, (q % 2) * 128 : (q % 2) * 128 + 128] = cg_all[q].astype(BF16)

    def cgz_copy(d):
        slot = cg_fin.at[c, z]
        return pltpu.make_async_remote_copy(
            slot, slot, cgz_s.at[d], cgz_r.at[d], device_id=column(d), device_id_type=MESH
        )

    def cgz_arrival(d):
        slot = cg_fin.at[c, zof(8 - d)]
        return pltpu.make_async_remote_copy(
            slot, slot, cgz_s.at[d], cgz_r.at[d], device_id=column(d), device_id_type=MESH
        )

    @pl.loop(1, 8)
    def _(d):
        cgz_copy(d).start()

    for cp in (p5f, q5f, p6f, q6f):
        cp.wait_recv()
    first_pass(blk(2, 2))

    target = 10.0 * total(mem[...] * protos[...].astype(F32))
    first = lax.broadcasted_iota(jnp.int32, (8, 256), 0) == 0
    stats[g, G : G + 8, :] = jnp.where(first, target, coarse_loss)

    def st_copy(d):
        return pltpu.make_async_remote_copy(
            stats.at[g], stats.at[g], st_s.at[d], st_r.at[d], device_id=plane(d), device_id_type=MESH
        )

    def st_arrival(d):
        slot = stats.at[lax.rem(g + G - d, G)]
        return pltpu.make_async_remote_copy(
            slot, slot, st_s.at[d], st_r.at[d], device_id=plane(d), device_id_type=MESH
        )

    @pl.loop(1, G)
    def _(d):
        st_copy(d).start()

    def core_copy(t):
        return pltpu.make_async_remote_copy(
            z_out.at[t, 1 - c], core_in.at[t], co_s.at[t], co_r.at[t], device_id=(other, g), device_id_type=MESH
        )

    def z_copy(t, d):
        return pltpu.make_async_remote_copy(
            z_out.at[t, c, zof(d)], z_in.at[t, d], zo_s.at[t, d], zo_r.at[t, d],
            device_id=column(d), device_id_type=MESH,
        )

    def za_copy(t, d):
        slot = fin.at[t, c, z]
        return pltpu.make_async_remote_copy(
            slot, slot, za_s.at[t, d], za_r.at[t, d], device_id=column(d), device_id_type=MESH
        )

    def za_arrival(t, d):
        slot = fin.at[t, c, zof(8 - d)]
        return pltpu.make_async_remote_copy(
            slot, slot, za_s.at[t, d], za_r.at[t, d], device_id=column(d), device_id_type=MESH
        )

    def ca_copy(t):
        slot = fin.at[t, c]
        return pltpu.make_async_remote_copy(
            slot, slot, ca_s.at[t], ca_r.at[t], device_id=(other, g), device_id_type=MESH
        )

    def ca_arrival(t):
        slot = fin.at[t, 1 - c]
        return pltpu.make_async_remote_copy(
            slot, slot, ca_s.at[t], ca_r.at[t], device_id=(other, g), device_id_type=MESH
        )

    def core_send(t, src):
        half = src[pl.ds(pl.multiple_of((1 - c) * 512, 512), 512), :].astype(BF16)
        z_out[t, 1 - c] = half.reshape(8, 64, D)
        core_copy(t).start()

    def core_merge(t, src):
        core_copy(t).wait_recv()
        half = src[pl.ds(pl.multiple_of(c * 512, 512), 512), :].reshape(8, 64, D)
        z_out[t, c] = (half + core_in[t].astype(F32)).astype(BF16)

        @pl.loop(1, 8)
        def _(d):
            z_copy(t, d).start()

    def z_merge(t):
        @pl.loop(1, 8)
        def _(d):
            z_copy(t, d).wait_recv()

        acc = z_out[t, c, z].astype(F32)
        for d in range(1, 8):
            acc = acc + z_in[t, d].astype(F32)
        fin[t, c, z] = acc.astype(BF16)

        @pl.loop(1, 8)
        def _(d):
            za_copy(t, d).start()

    def z_gathered(t):
        @pl.loop(1, 8)
        def _(d):
            za_arrival(t, d).wait_recv()

        ca_copy(t).start()

    core_send(0, mem)
    for j in range(NCH):
        rows = slice(j * 256, (j + 1) * 256)
        cpart[rows, :] = cpart_t[:, rows].T
    core_merge(0, mem)

    @pl.loop(1, G)
    def _(d):
        st_arrival(d).wait_recv()

    lse_peak = stats[0, 0:G, :]
    for j in range(1, G):
        lse_peak = jnp.maximum(lse_peak, stats[j, 0:G, :])
    lse_sum = jnp.zeros((G, 256), F32)
    extra = jnp.zeros((8, 256), F32)
    for j in range(G):
        lse_sum = lse_sum + jnp.exp(stats[j, 0:G, :] - lse_peak)
        extra = extra + stats[j, G : G + 8, :]
    log_total = lse_peak + jnp.log(lse_sum)
    wbuf[...] = jnp.exp(mmax[...] - log_total)
    loss_own = total(log_total) - extra[0:1, 0:1]
    coarse_all = extra[1:2, 0:1]

    def rw_copy(d):
        return pltpu.make_async_remote_copy(
            rout.at[d], rin.at[d], rw_s.at[d], rw_r.at[d], device_id=plane(d), device_id_type=MESH
        )

    def row_terms(i):
        return 10.0 * (obuf[i] * wbuf[pl.ds(i, 1), :] - lbuf[i].astype(F32))

    @pl.loop(1, G)
    def _(d):
        rout[d] = row_terms(lax.rem(g + d, G)).astype(BF16)
        rw_copy(d).start()

    own_rt[...] = row_terms(g)

    @pl.loop(0, G)
    def _(i):
        w_col = jnp.broadcast_to(wbuf[pl.ds(i, 1), :], (128, 256)).T
        for j in range(2):
            us[i, :, j * 128 : (j + 1) * 128] = (gbuf[i, :, j * 128 : (j + 1) * 128].astype(F32) * w_col).astype(BF16)

    for j in range(NCH):
        rows = slice(j * 256, (j + 1) * 256)
        soft[rows, :] = jnp.zeros((256, D), F32)

        @pl.loop(0, G)
        def _(i):
            soft[rows, :] += dot(ebuf[i, rows, :], us[i])

    core_send(1, soft)
    loss_core[0] = jnp.broadcast_to(loss_own, (8, 128))
    lcp = pltpu.make_async_remote_copy(
        loss_core.at[0], loss_core.at[1], ls_s.at[0], ls_r.at[0], device_id=(other, g), device_id_type=MESH
    )
    lcp.start()
    core_merge(1, soft)
    lcp.wait_recv()
    loss_z[0] = loss_core[0] + loss_core[1]

    def lz_copy(d):
        return pltpu.make_async_remote_copy(
            loss_z.at[0], loss_z.at[d], ls_s.at[d], ls_r.at[d], device_id=column(d), device_id_type=MESH
        )

    @pl.loop(1, 8)
    def _(d):
        lz_copy(d).start()

    @pl.loop(1, 8)
    def _(d):
        cgz_arrival(d).wait_recv()

    cg_mine, cg_theirs = cg_fin.at[c], cg_fin.at[1 - c]
    cgc = pltpu.make_async_remote_copy(
        cg_mine, cg_mine, cgz_s.at[0], cgz_r.at[0], device_id=(other, g), device_id_type=MESH
    )
    cgc_in = pltpu.make_async_remote_copy(
        cg_theirs, cg_theirs, cgz_s.at[0], cgz_r.at[0], device_id=(other, g), device_id_type=MESH
    )
    cgc.start()
    z_merge(0)
    cgc_in.wait_recv()
    o_cg[...] = cg_fin[...].reshape(KC, D).astype(F32)
    z_merge(1)
    z_gathered(0)
    ca_arrival(0).wait_recv()
    for j in range(NCH):
        rows = slice(j * 256, (j + 1) * 256)
        members = fin[0, j // 2, (j % 2) * 4 : (j % 2) * 4 + 4].reshape(256, D).astype(F32)
        p32 = protos[rows, :].astype(F32)
        norm = jnp.sqrt(jnp.sum(p32 * p32, axis=1, keepdims=True) + 1e-06)
        length = lax.rsqrt(jnp.sum(members * members, axis=1, keepdims=True) + 1e-06)
        o_new[rows, :] = 0.5 * p32 + (0.5 * norm) * (members * length)
        cpart[rows, :] = cpart[rows, :] - 2.5 * members

    acc = own_rt[...]
    for d in range(1, G):
        rw_copy(d).wait_recv()
        acc = acc + rin[d].astype(F32)
    own_rt[...] = acc
    row_grad = own_rt[...].T
    unit = unit_s[...]
    inv = inv_s[:, 0:1]
    o_emb[...] = inv * (row_grad - unit * jnp.sum(unit * row_grad, axis=1, keepdims=True))

    @pl.loop(1, 8)
    def _(d):
        lz_copy(d).wait_recv()

    fine = loss_z[0]
    for d in range(1, 8):
        fine = fine + loss_z[d]
    o_loss[...] = fine[0:1, 0:1] * (1.0 / (G * G * ROWS)) + coarse_all * (1.0 / (KL * G))

    z_gathered(1)
    ca_arrival(1).wait_recv()
    for j in range(NCH):
        rows = slice(j * 256, (j + 1) * 256)
        part = fin[1, j // 2, (j % 2) * 4 : (j % 2) * 4 + 4].reshape(256, D).astype(F32)
        o_pg[rows, :] = cpart[rows, :] + 2.5 * part

    for cp in sends + tails:
        cp.wait_send()

    @pl.loop(1, G)
    def _(d):
        lab_copy(d).wait_send()
        cgo_copy(d).wait_send()
        cga_copy(d).wait_send()
        st_copy(d).wait_send()
        rw_copy(d).wait_send()

    @pl.loop(1, 8)
    def _(d):
        cgz_copy(d).wait_send()
        lz_copy(d).wait_send()
        for t in range(2):
            z_copy(t, d).wait_send()
            za_copy(t, d).wait_send()

    cgc.wait_send()
    lcp.wait_send()
    for t in range(2):
        core_copy(t).wait_send()
        ca_copy(t).wait_send()


def body(embeddings, fine_labels, prototypes, coarse_protos, coarse_labels):
    vmem = pl.BlockSpec(memory_space=pltpu.VMEM)
    sem = pltpu.SemaphoreType.DMA
    scratch = [
        pltpu.VMEM((G, ROWS, D), BF16),
        pltpu.VMEM((G, 1, ROWS), jnp.int32),
        pltpu.VMEM((ROWS, D), F32),
        pltpu.VMEM((ROWS, 128), F32),
        pltpu.VMEM((D, KL), BF16),
        pltpu.VMEM((D, KC), BF16),
        pltpu.VMEM((KL, ROWS), F32),
        pltpu.VMEM((KL, ROWS), BF16),
        pltpu.VMEM((G, KL, ROWS), BF16),
        pltpu.VMEM((G, D, ROWS), F32),
        pltpu.VMEM((G, D, ROWS), BF16),
        pltpu.VMEM((G, ROWS, D), BF16),
        pltpu.VMEM((G, D, ROWS), BF16),
        pltpu.VMEM((G, D, ROWS), BF16),
        pltpu.VMEM((D, ROWS), F32),
        pltpu.VMEM((KL, D), F32),
        pltpu.VMEM((KL, D), F32),
        pltpu.VMEM((KC, D), F32),
        pltpu.VMEM((D, KL), F32),
        pltpu.VMEM((KL, D), F32),
        pltpu.VMEM((G, G + 8, ROWS), F32),
        pltpu.VMEM((G, ROWS), F32),
        pltpu.VMEM((G, ROWS), F32),
        pltpu.VMEM((G, 8, 128), F32),
        pltpu.VMEM((G, 8, 128), F32),
        pltpu.VMEM((G, 8, 128), F32),
        pltpu.VMEM((2, 8, 64, D), BF16),
        pltpu.VMEM((2, 8, 64, D), BF16),
        pltpu.VMEM((2, 2, 8, 64, D), BF16),
        pltpu.VMEM((2, 8, 64, D), BF16),
        pltpu.VMEM((2, 2, 8, 64, D), BF16),
        pltpu.VMEM((2, 8, 128), F32),
        pltpu.VMEM((8, 8, 128), F32),
        sem((N_GATHER,)), sem((N_GATHER,)),
        sem((G,)), sem((G,)), sem((G,)), sem((G,)), sem((G,)), sem((G,)),
        sem((8,)), sem((8,)),
        sem((G,)), sem((G,)), sem((G,)), sem((G,)),
        sem((2,)), sem((2,)),
        sem((2, 8)), sem((2, 8)), sem((2, 8)), sem((2, 8)),
        sem((2,)), sem((2,)),
        sem((8,)), sem((8,)),
    ]
    outs = [
        jax.ShapeDtypeStruct((ROWS, D), F32),
        jax.ShapeDtypeStruct((KL, D), F32),
        jax.ShapeDtypeStruct((KL, D), F32),
        jax.ShapeDtypeStruct((KC, D), F32),
        jax.ShapeDtypeStruct((1, 1), F32),
    ]
    ge, gp, new, gc, loss = pl.pallas_call(
        kernel,
        out_shape=outs,
        in_specs=[vmem] * 5,
        out_specs=[vmem] * 5,
        scratch_shapes=scratch,
        compiler_params=pltpu.CompilerParams(
            collective_id=0, has_side_effects=True, vmem_limit_bytes=56 * 1024 * 1024
        ),
    )(embeddings, fine_labels.reshape(1, ROWS), prototypes, coarse_protos, coarse_labels.reshape(NCH, 256))
    return ge, gp, new, gc, loss.reshape(())


def solution(mesh):
    in_specs = (P(("rows", "group"), None), P(("rows", "group")), P("group", None), P(), P("group"))
    out_specs = (P(("rows", "group"), None), P("group", None), P("group", None), P(), P())
    return jax.shard_map(body, mesh=mesh, in_specs=in_specs, out_specs=out_specs, check_vma=False)
```

```python
import functools

import jax
import jax.numpy as jnp
from jax import lax
from jax.experimental import pallas as pl
from jax.experimental.pallas import tpu as pltpu
from jax.sharding import PartitionSpec as P

MESH = pl.DeviceIdType.MESH
F32 = jnp.float32
BF16 = jnp.bfloat16
ROWS = 256
D = 256
KL = 1024
KC = 1024
G = 16
NCH = KL // 256
N_GATHER = 40
NT = (((1,), (1,)), ((), ()))
LOG2E = 1.4426950408889634


def dot(a, b):
    return jnp.dot(a, b, preferred_element_type=F32)


def dot_nt(a, b):
    return lax.dot_general(a, b, NT, preferred_element_type=F32)


def column_sum(value):
    return jnp.sum(value, axis=0, keepdims=True)


def total(value):
    return jnp.sum(jnp.sum(value, axis=0, keepdims=True), axis=1, keepdims=True)


def rel(dx, dy):
    return (dx % 4) * 4 + dy % 4


ORDER = [(0, 0), (1, 0), (3, 0), (0, 1), (0, 3), (1, 1), (1, 3), (3, 1), (3, 3), (0, 2), (1, 2), (3, 2)]
ORDER += [(2, 0), (2, 1), (2, 3), (2, 2)]
PEERS = ORDER[1:]
SLOT = {0: 0, 1: 1, 3: 2}


def kernel(
    emb, lab, protos, coarse, clab,
    o_emb, o_pg, o_new, o_cg, o_loss,
    gbuf, labs, unit_s, inv_s, protos_t, coarse_t, lscr, lscr2, ebuf, obuf, lbuf, us, rout, rin, own_rt,
    mem, soft, cg, cpart_t, cpart, stats_a, stats_b, mmax, lt_a, wbuf,
    cg_out, cg_in, cg_all, cg_fin, core_in, z_out, z_in, fin, extra, loss_core, loss_z,
    gs, gr, labs_s, labs_r, cgo_s, cgo_r, cga_s, cga_r, cgz_s, cgz_r, sa_s, sa_r, sb_s, sb_r, ex_s, ex_r,
    rw_s, rw_r, co_s, co_r, zo_s, zo_r, za_s, za_r, ca_s, ca_r, ls_s, ls_r,
):
    r = lax.axis_index("rows")
    g = lax.axis_index("group")
    z, c = r // 2, lax.rem(r, 2)
    x, y = g // 4, lax.rem(g, 4)
    other = r + 1 - 2 * c
    xs = [lax.rem(x + i, 4) * 4 for i in range(4)]
    ys = [lax.rem(y + i, 4) for i in range(4)]

    def plane(dx, dy):
        return (r, xs[dx % 4] + ys[dy % 4])

    def column(d):
        return (lax.rem(r + 2 * d, 16), g)

    def zof(d):
        return lax.rem(z + d, 8)

    barrier = pltpu.get_barrier_semaphore()
    for d in range(1, 8):
        pl.semaphore_signal(barrier, inc=1, device_id=column(d), device_id_type=MESH)
    for p in PEERS:
        pl.semaphore_signal(barrier, inc=1, device_id=plane(*p), device_id_type=MESH)
    pl.semaphore_signal(barrier, inc=1, device_id=(other, g), device_id_type=MESH)

    e32 = emb[...].astype(F32)
    inv = lax.rsqrt(jnp.sum(e32 * e32, axis=1, keepdims=True) + 1e-06)
    unit = e32 * inv
    unit_s[...] = unit
    inv_s[...] = jnp.broadcast_to(inv, (ROWS, 128))
    gbuf[0] = unit.astype(BF16)
    labs[0] = lab[...]

    pl.semaphore_wait(barrier, 23)

    A, B = (0, 128), (128, 128)
    A0, A1, B0, B1 = (0, 64), (64, 64), (128, 64), (192, 64)
    gathers = []

    def send(bx, by, rows, dx, dy):
        k = len(gathers)
        cp = pltpu.make_async_remote_copy(
            gbuf.at[rel(bx, by), pl.ds(*rows)], gbuf.at[rel(bx - dx, by - dy), pl.ds(*rows)],
            gs.at[k], gr.at[k], device_id=plane(dx, dy), device_id_type=MESH,
        )
        cp.start()
        gathers.append(cp)
        return cp

    def both_y(bx, by):
        return send(bx, by, A, 0, 1), send(bx, by, A, 0, 3)

    def both_x(bx, by):
        return send(bx, by, B, 1, 0), send(bx, by, B, 3, 0)

    def on_y(cp, bx, up):
        cp.wait_recv()
        return send(bx, 3, A0, 0, 1) if up else send(bx, 1, A1, 0, 3)

    def on_x(cp, by, up):
        cp.wait_recv()
        return send(3, by, B0, 1, 0) if up else send(1, by, B1, 3, 0)

    def arrived(*copies):
        for cp in copies:
            cp.wait_recv()

    def exchange(src, dst, send_sem, recv_sem):
        copies = []
        for k, p in enumerate(PEERS):
            cp = pltpu.make_async_remote_copy(
                src(k), dst(rel(-p[0], -p[1])), send_sem.at[k], recv_sem.at[k],
                device_id=plane(*p), device_id_type=MESH,
            )
            cp.start()
            copies.append(cp)
        return copies

    a1, a2 = send(0, 0, A, 1, 0), send(0, 0, A, 3, 0)
    b1, b2 = send(0, 0, B, 0, 1), send(0, 0, B, 0, 3)
    a3, a4 = both_y(0, 0)
    b3, b4 = both_x(0, 0)
    lab_x = exchange(lambda k: labs.at[0], lambda s: labs.at[s], labs_s, labs_r)

    iota = lax.broadcasted_iota(jnp.int32, (256, 256), 0)
    iota_half = iota.astype(F32).astype(BF16)
    parts = [slice(j * 256, (j + 1) * 256) for j in range(NCH)]

    for rows in parts:
        protos_t[:, rows] = protos[rows, :].astype(F32).T.astype(BF16)
        coarse_t[:, rows] = coarse[rows, :].astype(F32).T.astype(BF16)

    def logits_peak(left, u):
        peak = None
        for rows in parts:
            logits = dot_nt(left[rows, :], u)
            lscr[rows, :] = logits
            peak = logits if peak is None else jnp.maximum(peak, logits)
        return jnp.max(peak, axis=0, keepdims=True)

    def add(a, b):
        return b if a is None else a + b

    def onehot(labels, j):
        near = labels - j * 256
        near = jnp.where((near >= 0) & (near < 256), near, -1).astype(F32).astype(BF16)
        return jnp.where(iota_half == near, jnp.ones((), BF16), jnp.zeros((), BF16))

    def coarse_block(kb):
        u = protos[parts[kb], :]
        labels = clab[:, parts[kb]]
        peak = logits_peak(coarse, u)
        expsum = target = out = None
        for j, rows in enumerate(parts):
            logits = lscr[rows, :]
            target = add(target, jnp.where(iota == labels - j * 256, logits, 0.0))
            e = jnp.exp2((logits - peak) * (10.0 * LOG2E))
            expsum = add(expsum, e)
            lscr2[rows, :] = e
        expsum = column_sum(expsum)
        share = 10.0 / expsum
        for j, rows in enumerate(parts):
            delta = (lscr2[rows, :] * share - jnp.where(iota == labels - j * 256, 10.0, 0.0)).astype(BF16)
            out = add(out, dot(coarse_t[:, rows], delta))
            if kb == 0:
                cg[rows, :] = dot(delta, u)
            else:
                cg[rows, :] += dot(delta, u)
        cpart_t[:, parts[kb]] = out
        return total(10.0 * (peak - column_sum(target)) + jnp.log(expsum))

    def local_labels(p):
        return labs[rel(*p)] - g * KL

    def first_pass(k, prev):
        dx, dy = ORDER[k]
        u = gbuf[rel(dx, dy)]
        peak = logits_peak(protos, u)
        labels = local_labels(ORDER[k])
        expsum = out = None
        for j, rows in enumerate(parts):
            e = jnp.exp2((lscr[rows, :] - peak) * (10.0 * LOG2E))
            expsum = add(expsum, e)
            ebuf[k, rows, :] = e.astype(BF16)
            if prev is not None:
                out = add(out, dot(protos_t[:, rows], ebuf[prev, rows, :]))
            member = dot(onehot(labels, j), u)
            if k == 0:
                mem[rows, :] = member
            else:
                mem[rows, :] += member
        if prev is not None:
            obuf[prev] = out
        mmax[k : k + 1, :] = 10.0 * peak
        lse = 10.0 * peak + jnp.log(column_sum(expsum))
        if dx == 2:
            stats_b[0, pl.ds(ys[dy], 1), :] = lse
        else:
            stats_a[0, pl.ds(SLOT[dx] * 4 + ys[dy], 1), :] = lse

    coarse_loss = coarse_block(0)
    first_pass(0, None)

    a1.wait_recv()
    f1 = send(3, 0, A0, 1, 0)
    p1, p2 = both_y(3, 0)
    b1.wait_recv()
    g1 = send(0, 3, B0, 0, 1)
    q1, q2 = both_x(0, 3)
    a2.wait_recv()
    f2 = send(1, 0, A1, 3, 0)
    p3, p4 = both_y(1, 0)
    b2.wait_recv()
    g2 = send(0, 1, B1, 0, 3)
    q3, q4 = both_x(0, 1)
    coarse_loss = coarse_loss + coarse_block(1)
    a3f, b3f, a4f, b4f = on_y(a3, 0, True), on_x(b3, 0, True), on_y(a4, 0, False), on_x(b4, 0, False)
    coarse_loss = coarse_loss + coarse_block(2)
    coarse_loss = coarse_loss + coarse_block(3)

    base = c * 512 + z * 64

    def tile_of(q):
        return cg[pl.ds(pl.multiple_of(base + 8 * (q // 2), 8), 8), (q % 2) * 128 : (q % 2) * 128 + 128]

    for q in range(G):
        cg_out[q] = tile_of(q)
    cgo_x = []
    for k, p in enumerate(PEERS):
        cp = pltpu.make_async_remote_copy(
            cg_out.at[xs[p[0]] + ys[p[1]]], cg_in.at[k], cgo_s.at[k], cgo_r.at[k],
            device_id=plane(*p), device_id_type=MESH,
        )
        cp.start()
        cgo_x.append(cp)

    arrived(*lab_x)
    arrived(f1, f2)
    p5, p6 = both_y(2, 0)
    arrived(g1, g2)
    q5, q6 = both_x(0, 2)
    first_pass(1, 0)
    first_pass(2, 1)
    p1f, q1f, p2f, q2f = on_y(p1, 3, True), on_x(q1, 3, True), on_y(p2, 3, False), on_x(q2, 3, False)
    first_pass(3, 2)
    p3f, q3f, p4f, q4f = on_y(p3, 1, True), on_x(q3, 1, True), on_y(p4, 1, False), on_x(q4, 1, False)
    first_pass(4, 3)
    first_pass(5, 4)
    p5f, q5f, p6f, q6f = on_y(p5, 2, True), on_x(q5, 2, True), on_y(p6, 2, False), on_x(q6, 2, False)
    first_pass(6, 5)
    first_pass(7, 6)
    first_pass(8, 7)

    arrived(*cgo_x)
    tile = cg_out[g]
    for k in range(G - 1):
        tile = tile + cg_in[k]
    cg_all[g] = (KC / (KL * G)) * tile
    cga_x = []
    for k, p in enumerate(PEERS):
        cp = pltpu.make_async_remote_copy(
            cg_all.at[g], cg_all.at[g], cga_s.at[k], cga_r.at[k], device_id=plane(*p), device_id_type=MESH
        )
        cp.start()
        cga_x.append(cp)

    arrived(a3f, b3f, a4f, b4f)
    first_pass(9, 8)
    arrived(p1f, p2f, p3f, p4f)
    first_pass(10, 9)
    first_pass(11, 10)
    sa_x = exchange(lambda k: stats_a.at[0], lambda s: stats_a.at[s], sa_s, sa_r)
    first_pass(12, 11)
    arrived(q1f, q2f, q3f, q4f)
    first_pass(13, 12)
    first_pass(14, 13)

    arrived(*cga_x)
    for q in range(G):
        cg_fin[c, z, (q // 2) * 8 : (q // 2) * 8 + 8, (q % 2) * 128 : (q % 2) * 128 + 128] = cg_all[q].astype(BF16)

    @functools.cache
    def cgz_copy(d):
        slot = cg_fin.at[c, z]
        return pltpu.make_async_remote_copy(
            slot, slot, cgz_s.at[d], cgz_r.at[d], device_id=column(d), device_id_type=MESH
        )

    for d in range(1, 8):
        cgz_copy(d).start()

    arrived(p5f, q5f, p6f, q6f)
    first_pass(15, 14)
    sb_x = exchange(lambda k: stats_b.at[0], lambda s: stats_b.at[s], sb_s, sb_r)

    @functools.cache
    def core_copy(t):
        return pltpu.make_async_remote_copy(
            z_out.at[t, 1 - c], core_in.at[t], co_s.at[t], co_r.at[t], device_id=(other, g), device_id_type=MESH
        )

    @functools.cache
    def z_copy(t, d):
        return pltpu.make_async_remote_copy(
            z_out.at[t, c, zof(d)], z_in.at[t, d], zo_s.at[t, d], zo_r.at[t, d],
            device_id=column(d), device_id_type=MESH,
        )

    @functools.cache
    def za_copy(t, d):
        slot = fin.at[t, c, z]
        return pltpu.make_async_remote_copy(
            slot, slot, za_s.at[t, d], za_r.at[t, d], device_id=column(d), device_id_type=MESH
        )

    @functools.cache
    def ca_copy(t):
        slot = fin.at[t, c]
        return pltpu.make_async_remote_copy(
            slot, slot, ca_s.at[t], ca_r.at[t], device_id=(other, g), device_id_type=MESH
        )

    def core_send(t, src):
        half = src[pl.ds(pl.multiple_of((1 - c) * 512, 512), 512), :].astype(BF16)
        z_out[t, 1 - c] = half.reshape(8, 64, D)
        core_copy(t).start()

    def core_merge(t, src):
        core_copy(t).wait_recv()
        half = src[pl.ds(pl.multiple_of(c * 512, 512), 512), :].reshape(8, 64, D)
        z_out[t, c] = (half + core_in[t].astype(F32)).astype(BF16)

        for d in range(1, 8):
            z_copy(t, d).start()

    def z_merge(t):
        for d in range(1, 8):
            z_copy(t, d).wait_recv()

        acc = z_out[t, c, z].astype(F32)
        for d in range(1, 8):
            acc = acc + z_in[t, d].astype(F32)
        fin[t, c, z] = acc.astype(BF16)

        for d in range(1, 8):
            za_copy(t, d).start()

    def z_gathered(t):
        for d in range(1, 8):
            za_copy(t, d).wait_recv()

        ca_copy(t).start()

    core_send(0, mem)
    target = 10.0 * total(mem[...] * protos[...].astype(F32))
    first = lax.broadcasted_iota(jnp.int32, (8, 128), 0) == 0
    extra[0] = jnp.where(first, target, coarse_loss)
    ex_x = exchange(lambda k: extra.at[0], lambda s: extra.at[s], ex_s, ex_r)
    core_merge(0, mem)

    last = None
    for rows in parts:
        last = add(last, dot(protos_t[:, rows], ebuf[15, rows, :]))
    obuf[15] = last
    for k, p in enumerate(ORDER):
        labels = local_labels(p)
        out = None
        for j, rows in enumerate(parts):
            out = add(out, dot(protos_t[:, rows], onehot(labels, j)))
        lbuf[k] = out.astype(BF16)
    for rows in parts:
        cpart[rows, :] = cpart_t[:, rows].T

    arrived(*sa_x)
    arrived(*sb_x)

    def line(a, b, dx):
        away = (dx - a) % 4
        if away == 2:
            return stats_b[rel(a, b)]
        return stats_a[rel(a, b), SLOT[away] * 4 : SLOT[away] * 4 + 4, :]

    loss_rows = None
    for dx in range(4):
        lines = [line(a, b, dx) for a in range(4) for b in range(4)]
        peak = functools.reduce(jnp.maximum, lines)
        log_total = peak + jnp.log(functools.reduce(add, [jnp.exp(v - peak) for v in lines]))
        lt_a[dx] = log_total
        loss_rows = add(loss_rows, log_total)
    for k, (dx, dy) in enumerate(ORDER):
        wbuf[k : k + 1, :] = jnp.exp(mmax[k : k + 1, :] - lt_a[dx, pl.ds(ys[dy], 1), :])

    def row_terms(k):
        return 10.0 * (obuf[k] * wbuf[k : k + 1, :] - lbuf[k].astype(F32))

    rw_x = []
    for k in range(G - 1, 0, -1):
        p = ORDER[k]
        rout[k] = row_terms(k).astype(BF16)
        cp = pltpu.make_async_remote_copy(
            rout.at[k], rin.at[k], rw_s.at[k], rw_r.at[k], device_id=plane(*p), device_id_type=MESH
        )
        cp.start()
        rw_x.append(cp)
    own_rt[...] = row_terms(0)

    for j, rows in enumerate(parts):
        acc = None
        for k, p in enumerate(ORDER):
            if j == 0:
                w_col = jnp.broadcast_to(wbuf[k : k + 1, :], (128, 256)).T
                for h in (slice(0, 128), slice(128, 256)):
                    us[k, :, h] = (gbuf[rel(*p), :, h].astype(F32) * w_col).astype(BF16)
            acc = add(acc, dot(ebuf[k, rows, :], us[k]))
        soft[rows, :] = acc

    core_send(1, soft)
    arrived(*ex_x)
    sums = functools.reduce(add, [extra[k] for k in range(G)])
    coarse_all = sums[1:2, 0:1]
    loss_core[0] = jnp.broadcast_to(total(loss_rows) - sums[0:1, 0:1], (8, 128))
    lcp = pltpu.make_async_remote_copy(
        loss_core.at[0], loss_core.at[1], ls_s.at[0], ls_r.at[0], device_id=(other, g), device_id_type=MESH
    )
    lcp.start()
    core_merge(1, soft)
    lcp.wait_recv()
    loss_z[0] = loss_core[0] + loss_core[1]

    @functools.cache
    def lz_copy(d):
        return pltpu.make_async_remote_copy(
            loss_z.at[0], loss_z.at[d], ls_s.at[d], ls_r.at[d], device_id=column(d), device_id_type=MESH
        )

    for d in range(1, 8):
        lz_copy(d).start()

    for d in range(1, 8):
        cgz_copy(d).wait_recv()

    cg_mine = cg_fin.at[c]
    cgc = pltpu.make_async_remote_copy(
        cg_mine, cg_mine, cgz_s.at[0], cgz_r.at[0], device_id=(other, g), device_id_type=MESH
    )
    cgc.start()
    z_merge(0)
    cgc.wait_recv()
    o_cg[...] = cg_fin[...].reshape(KC, D).astype(F32)
    z_merge(1)
    z_gathered(0)
    ca_copy(0).wait_recv()
    for j, rows in enumerate(parts):
        members = fin[0, j // 2, (j % 2) * 4 : (j % 2) * 4 + 4].reshape(256, D).astype(F32)
        p32 = protos[rows, :].astype(F32)
        norm = jnp.sqrt(jnp.sum(p32 * p32, axis=1, keepdims=True) + 1e-06)
        length = lax.rsqrt(jnp.sum(members * members, axis=1, keepdims=True) + 1e-06)
        o_new[rows, :] = 0.5 * p32 + (0.5 * norm) * (members * length)
        cpart[rows, :] = cpart[rows, :] - 2.5 * members

    arrived(*rw_x)
    acc = own_rt[...]
    for k in range(1, G):
        acc = acc + rin[k].astype(F32)
    row_grad = acc.T
    unit = unit_s[...]
    inv = inv_s[:, 0:1]
    o_emb[...] = inv * (row_grad - unit * jnp.sum(unit * row_grad, axis=1, keepdims=True))

    for d in range(1, 8):
        lz_copy(d).wait_recv()

    fine = functools.reduce(add, [loss_z[d] for d in range(8)])
    o_loss[...] = fine[0:1, 0:1] * (1.0 / (G * G * ROWS)) + coarse_all * (1.0 / (KL * G))

    z_gathered(1)
    ca_copy(1).wait_recv()
    for j, rows in enumerate(parts):
        part = fin[1, j // 2, (j % 2) * 4 : (j % 2) * 4 + 4].reshape(256, D).astype(F32)
        o_pg[rows, :] = cpart[rows, :] + 2.5 * part

    for cp in gathers + lab_x + cgo_x + cga_x + sa_x + sb_x + ex_x + rw_x:
        cp.wait_send()

    for d in range(1, 8):
        cgz_copy(d).wait_send()
        lz_copy(d).wait_send()
        for t in range(2):
            z_copy(t, d).wait_send()
            za_copy(t, d).wait_send()

    cgc.wait_send()
    lcp.wait_send()
    for t in range(2):
        core_copy(t).wait_send()
        ca_copy(t).wait_send()


def body(embeddings, fine_labels, prototypes, coarse_protos, coarse_labels):
    vmem = pl.BlockSpec(memory_space=pltpu.VMEM)
    sem = pltpu.SemaphoreType.DMA
    scratch = [
        pltpu.VMEM((G, ROWS, D), BF16),
        pltpu.VMEM((G, 1, ROWS), jnp.int32),
        pltpu.VMEM((ROWS, D), F32),
        pltpu.VMEM((ROWS, 128), F32),
        pltpu.VMEM((D, KL), BF16),
        pltpu.VMEM((D, KC), BF16),
        pltpu.VMEM((KL, ROWS), F32),
        pltpu.VMEM((KL, ROWS), F32),
        pltpu.VMEM((G, KL, ROWS), BF16),
        pltpu.VMEM((G, D, ROWS), F32),
        pltpu.VMEM((G, D, ROWS), BF16),
        pltpu.VMEM((G, ROWS, D), BF16),
        pltpu.VMEM((G, D, ROWS), BF16),
        pltpu.VMEM((G, D, ROWS), BF16),
        pltpu.VMEM((D, ROWS), F32),
        pltpu.VMEM((KL, D), F32),
        pltpu.VMEM((KL, D), F32),
        pltpu.VMEM((KC, D), F32),
        pltpu.VMEM((D, KL), F32),
        pltpu.VMEM((KL, D), F32),
        pltpu.VMEM((G, 16, ROWS), F32),
        pltpu.VMEM((G, 4, ROWS), F32),
        pltpu.VMEM((G, ROWS), F32),
        pltpu.VMEM((4, 4, ROWS), F32),
        pltpu.VMEM((G, ROWS), F32),
        pltpu.VMEM((G, 8, 128), F32),
        pltpu.VMEM((G, 8, 128), F32),
        pltpu.VMEM((G, 8, 128), F32),
        pltpu.VMEM((2, 8, 64, D), BF16),
        pltpu.VMEM((2, 8, 64, D), BF16),
        pltpu.VMEM((2, 2, 8, 64, D), BF16),
        pltpu.VMEM((2, 8, 64, D), BF16),
        pltpu.VMEM((2, 2, 8, 64, D), BF16),
        pltpu.VMEM((G, 8, 128), F32),
        pltpu.VMEM((2, 8, 128), F32),
        pltpu.VMEM((8, 8, 128), F32),
        sem((N_GATHER,)), sem((N_GATHER,)),
        sem((G,)), sem((G,)), sem((G,)), sem((G,)), sem((G,)), sem((G,)),
        sem((8,)), sem((8,)),
        sem((G,)), sem((G,)), sem((G,)), sem((G,)), sem((G,)), sem((G,)), sem((G,)), sem((G,)),
        sem((2,)), sem((2,)),
        sem((2, 8)), sem((2, 8)), sem((2, 8)), sem((2, 8)),
        sem((2,)), sem((2,)),
        sem((8,)), sem((8,)),
    ]
    outs = [
        pltpu.VMEM((ROWS, D), F32),
        pltpu.VMEM((KL, D), F32),
        pltpu.VMEM((KL, D), F32),
        pltpu.VMEM((KC, D), F32),
        jax.ShapeDtypeStruct((1, 1), F32),
    ]
    ge, gp, new, gc, loss = pl.pallas_call(
        kernel,
        out_shape=outs,
        in_specs=[vmem] * 5,
        out_specs=[vmem] * 5,
        scratch_shapes=scratch,
        compiler_params=pltpu.CompilerParams(
            collective_id=0, has_side_effects=True, vmem_limit_bytes=56 * 1024 * 1024
        ),
    )(embeddings, fine_labels.reshape(1, ROWS), prototypes, coarse_protos, coarse_labels.reshape(1, KC))
    return ge, gp, new, gc, loss.reshape(())


def solution(mesh):
    in_specs = (P(("rows", "group"), None), P(("rows", "group")), P("group", None), P(), P("group"))
    out_specs = (P(("rows", "group"), None), P("group", None), P("group", None), P(), P())
    return jax.shard_map(body, mesh=mesh, in_specs=in_specs, out_specs=out_specs, check_vma=False)
```

```python
import functools

import jax
import jax.numpy as jnp
from jax import lax
from jax.experimental import pallas as pl
from jax.experimental.pallas import tpu as pltpu
from jax.sharding import PartitionSpec as P

MESH = pl.DeviceIdType.MESH
F32 = jnp.float32
BF16 = jnp.bfloat16
ROWS = 256
D = 256
KL = 1024
KC = 1024
G = 16
NCH = KL // 256
N_GATHER = 40
NT = (((1,), (1,)), ((), ()))
LOG2E = 1.4426950408889634


def dot(a, b):
    return jnp.dot(a, b, preferred_element_type=F32)


def dot_nt(a, b):
    return lax.dot_general(a, b, NT, preferred_element_type=F32)


def column_sum(value):
    return jnp.sum(value, axis=0, keepdims=True)


def total(value):
    return jnp.sum(jnp.sum(value, axis=0, keepdims=True), axis=1, keepdims=True)


def rel(dx, dy):
    return (dx % 4) * 4 + dy % 4


ORDER = [(0, 0), (1, 0), (3, 0), (0, 1), (0, 3), (1, 1), (1, 3), (3, 1), (3, 3), (0, 2), (1, 2), (3, 2)]
ORDER += [(2, 0), (2, 1), (2, 3), (2, 2)]
PEERS = ORDER[1:]
SLOT = {0: 0, 1: 1, 3: 2}


def kernel(
    emb, lab, protos, coarse, clab,
    o_emb, o_pg, o_new, o_cg, o_loss,
    gbuf, labs, unit_s, inv_s, protos_t, coarse_t, lscr, lscr2, ebuf, obuf, lbuf, us, rout, rin, own_rt,
    mem, soft, cg, cpart_t, cpart, stats_a, stats_b, mmax, lt_a, wbuf,
    cg_out, cg_in, cg_all, cg_fin, core_in, z_out, z_in, fin, loss_core, loss_z,
    gs, gr, labs_s, labs_r, cgo_s, cgo_r, cga_s, cga_r, cgz_s, cgz_r, sa_s, sa_r, sb_s, sb_r,
    rw_s, rw_r, co_s, co_r, zo_s, zo_r, za_s, za_r, ca_s, ca_r, ls_s, ls_r,
):
    r = lax.axis_index("rows")
    g = lax.axis_index("group")
    z, c = r // 2, lax.rem(r, 2)
    x, y = g // 4, lax.rem(g, 4)
    other = r + 1 - 2 * c
    xs = [lax.rem(x + i, 4) * 4 for i in range(4)]
    ys = [lax.rem(y + i, 4) for i in range(4)]

    def plane(dx, dy):
        return (r, xs[dx % 4] + ys[dy % 4])

    def column(d):
        return (lax.rem(r + 2 * d, 16), g)

    def zof(d):
        return lax.rem(z + d, 8)

    barrier = pltpu.get_barrier_semaphore()
    for d in range(1, 8):
        pl.semaphore_signal(barrier, inc=1, device_id=column(d), device_id_type=MESH)
    for p in PEERS:
        pl.semaphore_signal(barrier, inc=1, device_id=plane(*p), device_id_type=MESH)
    pl.semaphore_signal(barrier, inc=1, device_id=(other, g), device_id_type=MESH)

    e32 = emb[...].astype(F32)
    inv = lax.rsqrt(jnp.sum(e32 * e32, axis=1, keepdims=True) + 1e-06)
    unit = e32 * inv
    unit_s[...] = unit
    inv_s[...] = jnp.broadcast_to(inv, (ROWS, 128))
    gbuf[0] = unit.astype(BF16)
    labs[0] = lab[...]

    pl.semaphore_wait(barrier, 23)

    A, B = (0, 128), (128, 128)
    A0, A1, B0, B1 = (0, 64), (64, 64), (128, 64), (192, 64)
    gathers = []

    def send(bx, by, rows, dx, dy):
        k = len(gathers)
        cp = pltpu.make_async_remote_copy(
            gbuf.at[rel(bx, by), pl.ds(*rows)], gbuf.at[rel(bx - dx, by - dy), pl.ds(*rows)],
            gs.at[k], gr.at[k], device_id=plane(dx, dy), device_id_type=MESH,
        )
        cp.start()
        gathers.append(cp)
        return cp

    def both_y(bx, by):
        return send(bx, by, A, 0, 1), send(bx, by, A, 0, 3)

    def both_x(bx, by):
        return send(bx, by, B, 1, 0), send(bx, by, B, 3, 0)

    def on_y(cp, bx, up):
        cp.wait_recv()
        return send(bx, 3, A0, 0, 1) if up else send(bx, 1, A1, 0, 3)

    def on_x(cp, by, up):
        cp.wait_recv()
        return send(3, by, B0, 1, 0) if up else send(1, by, B1, 3, 0)

    def arrived(*copies):
        for cp in copies:
            cp.wait_recv()

    def exchange(src, dst, send_sem, recv_sem):
        copies = []
        for k, p in enumerate(PEERS):
            cp = pltpu.make_async_remote_copy(
                src(k), dst(rel(-p[0], -p[1])), send_sem.at[k], recv_sem.at[k],
                device_id=plane(*p), device_id_type=MESH,
            )
            cp.start()
            copies.append(cp)
        return copies

    a1, a2 = send(0, 0, A, 1, 0), send(0, 0, A, 3, 0)
    b1, b2 = send(0, 0, B, 0, 1), send(0, 0, B, 0, 3)
    a3, a4 = both_y(0, 0)
    b3, b4 = both_x(0, 0)
    lab_x = exchange(lambda k: labs.at[0], lambda s: labs.at[s], labs_s, labs_r)

    iota = lax.broadcasted_iota(jnp.int32, (256, 256), 0)
    iota_half = iota.astype(F32).astype(BF16)
    parts = [slice(j * 256, (j + 1) * 256) for j in range(NCH)]

    for rows in parts:
        protos_t[:, rows] = protos[rows, :].astype(F32).T.astype(BF16)
        coarse_t[:, rows] = coarse[rows, :].astype(F32).T.astype(BF16)

    def logits_peak(left, u):
        peak = None
        for rows in parts:
            logits = dot_nt(left[rows, :], u)
            lscr[rows, :] = logits
            peak = logits if peak is None else jnp.maximum(peak, logits)
        return jnp.max(peak, axis=0, keepdims=True)

    def add(a, b):
        return b if a is None else a + b

    def onehot(labels, j):
        near = labels - j * 256
        near = jnp.where((near >= 0) & (near < 256), near, -1).astype(F32).astype(BF16)
        return jnp.where(iota_half == near, jnp.ones((), BF16), jnp.zeros((), BF16))

    def coarse_block(kb):
        u = protos[parts[kb], :]
        labels = clab[:, parts[kb]]
        peak = logits_peak(coarse, u)
        expsum = target = out = None
        for j, rows in enumerate(parts):
            logits = lscr[rows, :]
            target = add(target, jnp.where(iota == labels - j * 256, logits, 0.0))
            e = jnp.exp2((logits - peak) * (10.0 * LOG2E))
            expsum = add(expsum, e)
            lscr2[rows, :] = e
        expsum = column_sum(expsum)
        share = 10.0 / expsum
        for j, rows in enumerate(parts):
            delta = (lscr2[rows, :] * share - jnp.where(iota == labels - j * 256, 10.0, 0.0)).astype(BF16)
            out = add(out, dot(coarse_t[:, rows], delta))
            if kb == 0:
                cg[rows, :] = dot(delta, u)
            else:
                cg[rows, :] += dot(delta, u)
        cpart_t[:, parts[kb]] = out
        return total(10.0 * (peak - column_sum(target)) + jnp.log(expsum))

    def local_labels(p):
        return labs[rel(*p)] - g * KL

    def first_pass(k, prev):
        dx, dy = ORDER[k]
        u = gbuf[rel(dx, dy)]
        peak = logits_peak(protos, u)
        labels = local_labels(ORDER[k])
        expsum = out = None
        for j, rows in enumerate(parts):
            e = jnp.exp2((lscr[rows, :] - peak) * (10.0 * LOG2E))
            expsum = add(expsum, e)
            ebuf[k, rows, :] = e.astype(BF16)
            if prev is not None:
                out = add(out, dot(protos_t[:, rows], ebuf[prev, rows, :]))
            member = dot(onehot(labels, j), u)
            if k == 0:
                mem[rows, :] = member
            else:
                mem[rows, :] += member
        if prev is not None:
            obuf[prev] = out
        mmax[k : k + 1, :] = 10.0 * peak
        lse = 10.0 * peak + jnp.log(column_sum(expsum))
        if dx == 2:
            stats_b[0, pl.ds(ys[dy], 1), :] = lse
        else:
            stats_a[0, pl.ds(SLOT[dx] * 4 + ys[dy], 1), :] = lse

    def label_rows(*which):
        for k in which:
            labels = local_labels(ORDER[k])
            out = None
            for j, rows in enumerate(parts):
                out = add(out, dot(protos_t[:, rows], onehot(labels, j)))
            lbuf[k] = out.astype(BF16)

    coarse_loss = coarse_block(0)
    first_pass(0, None)

    a1.wait_recv()
    f1 = send(3, 0, A0, 1, 0)
    p1, p2 = both_y(3, 0)
    b1.wait_recv()
    g1 = send(0, 3, B0, 0, 1)
    q1, q2 = both_x(0, 3)
    a2.wait_recv()
    f2 = send(1, 0, A1, 3, 0)
    p3, p4 = both_y(1, 0)
    b2.wait_recv()
    g2 = send(0, 1, B1, 0, 3)
    q3, q4 = both_x(0, 1)
    coarse_loss = coarse_loss + coarse_block(1)
    a3f, b3f, a4f, b4f = on_y(a3, 0, True), on_x(b3, 0, True), on_y(a4, 0, False), on_x(b4, 0, False)
    coarse_loss = coarse_loss + coarse_block(2)
    coarse_loss = coarse_loss + coarse_block(3)

    base = c * 512 + z * 64

    def tile_of(q):
        return cg[pl.ds(pl.multiple_of(base + 8 * (q // 2), 8), 8), (q % 2) * 128 : (q % 2) * 128 + 128]

    for q in range(G):
        cg_out[q] = tile_of(q)
    cgo_x = []
    for k, p in enumerate(PEERS):
        cp = pltpu.make_async_remote_copy(
            cg_out.at[xs[p[0]] + ys[p[1]]], cg_in.at[k], cgo_s.at[k], cgo_r.at[k],
            device_id=plane(*p), device_id_type=MESH,
        )
        cp.start()
        cgo_x.append(cp)

    arrived(*lab_x)
    arrived(f1, f2)
    p5, p6 = both_y(2, 0)
    arrived(g1, g2)
    q5, q6 = both_x(0, 2)
    first_pass(1, 0)
    first_pass(2, 1)
    p1f, q1f, p2f, q2f = on_y(p1, 3, True), on_x(q1, 3, True), on_y(p2, 3, False), on_x(q2, 3, False)
    first_pass(3, 2)
    p3f, q3f, p4f, q4f = on_y(p3, 1, True), on_x(q3, 1, True), on_y(p4, 1, False), on_x(q4, 1, False)
    first_pass(4, 3)
    first_pass(5, 4)
    p5f, q5f, p6f, q6f = on_y(p5, 2, True), on_x(q5, 2, True), on_y(p6, 2, False), on_x(q6, 2, False)
    first_pass(6, 5)
    first_pass(7, 6)
    first_pass(8, 7)

    arrived(*cgo_x)
    tile = cg_out[g]
    for k in range(G - 1):
        tile = tile + cg_in[k]
    cg_all[g] = (KC / (KL * G)) * tile
    cga_x = []
    for k, p in enumerate(PEERS):
        cp = pltpu.make_async_remote_copy(
            cg_all.at[g], cg_all.at[g], cga_s.at[k], cga_r.at[k], device_id=plane(*p), device_id_type=MESH
        )
        cp.start()
        cga_x.append(cp)

    label_rows(0, 1, 2)
    arrived(a3f, b3f, a4f, b4f)
    first_pass(9, 8)
    arrived(p1f, p2f, p3f, p4f)
    first_pass(10, 9)
    first_pass(11, 10)
    sa_x = exchange(lambda k: stats_a.at[0], lambda s: stats_a.at[s], sa_s, sa_r)
    first_pass(12, 11)
    label_rows(3, 4, 5)
    arrived(q1f, q2f, q3f, q4f)
    first_pass(13, 12)
    first_pass(14, 13)

    arrived(*cga_x)
    for q in range(G):
        cg_fin[c, z, (q // 2) * 8 : (q // 2) * 8 + 8, (q % 2) * 128 : (q % 2) * 128 + 128] = cg_all[q].astype(BF16)

    @functools.cache
    def cgz_copy(d):
        slot = cg_fin.at[c, z]
        return pltpu.make_async_remote_copy(
            slot, slot, cgz_s.at[d], cgz_r.at[d], device_id=column(d), device_id_type=MESH
        )

    for d in range(1, 8):
        cgz_copy(d).start()

    label_rows(6, 7, 8, 9)
    arrived(p5f, q5f, p6f, q6f)
    first_pass(15, 14)
    target = 10.0 * total(mem[...] * protos[...].astype(F32))
    head = lax.broadcasted_iota(jnp.int32, (4, ROWS), 0) == 0
    stats_b[0, 4:8, :] = jnp.where(head, target, coarse_loss)
    sb_x = exchange(lambda k: stats_b.at[0], lambda s: stats_b.at[s], sb_s, sb_r)

    @functools.cache
    def core_copy(t):
        return pltpu.make_async_remote_copy(
            z_out.at[t, 1 - c], core_in.at[t], co_s.at[t], co_r.at[t], device_id=(other, g), device_id_type=MESH
        )

    @functools.cache
    def z_copy(t, d):
        return pltpu.make_async_remote_copy(
            z_out.at[t, c, zof(d)], z_in.at[t, d], zo_s.at[t, d], zo_r.at[t, d],
            device_id=column(d), device_id_type=MESH,
        )

    @functools.cache
    def za_copy(t, d):
        slot = fin.at[t, c, z]
        return pltpu.make_async_remote_copy(
            slot, slot, za_s.at[t, d], za_r.at[t, d], device_id=column(d), device_id_type=MESH
        )

    @functools.cache
    def ca_copy(t):
        slot = fin.at[t, c]
        return pltpu.make_async_remote_copy(
            slot, slot, ca_s.at[t], ca_r.at[t], device_id=(other, g), device_id_type=MESH
        )

    def core_send(t, src):
        half = src[pl.ds(pl.multiple_of((1 - c) * 512, 512), 512), :].astype(BF16)
        z_out[t, 1 - c] = half.reshape(8, 64, D)
        core_copy(t).start()

    def core_merge(t, src):
        core_copy(t).wait_recv()
        half = src[pl.ds(pl.multiple_of(c * 512, 512), 512), :].reshape(8, 64, D)
        z_out[t, c] = (half + core_in[t].astype(F32)).astype(BF16)

        for d in range(1, 8):
            z_copy(t, d).start()

    def z_merge(t):
        for d in range(1, 8):
            z_copy(t, d).wait_recv()

        acc = z_out[t, c, z].astype(F32)
        for d in range(1, 8):
            acc = acc + z_in[t, d].astype(F32)
        fin[t, c, z] = acc.astype(BF16)

        for d in range(1, 8):
            za_copy(t, d).start()

    def z_gathered(t):
        for d in range(1, 8):
            za_copy(t, d).wait_recv()

        ca_copy(t).start()

    core_send(0, mem)
    core_merge(0, mem)

    last = None
    for rows in parts:
        last = add(last, dot(protos_t[:, rows], ebuf[15, rows, :]))
    obuf[15] = last
    label_rows(10, 11, 12, 13, 14, 15)

    arrived(*sa_x)
    arrived(*sb_x)

    def line(a, b, dx):
        away = (dx - a) % 4
        if away == 2:
            return stats_b[rel(a, b), 0:4, :]
        return stats_a[rel(a, b), SLOT[away] * 4 : SLOT[away] * 4 + 4, :]

    loss_rows = None
    for dx in range(4):
        lines = [line(a, b, dx) for a in range(4) for b in range(4)]
        peak = functools.reduce(jnp.maximum, lines)
        log_total = peak + jnp.log(functools.reduce(add, [jnp.exp(v - peak) for v in lines]))
        lt_a[dx] = log_total
        loss_rows = add(loss_rows, log_total)
    for k, (dx, dy) in enumerate(ORDER):
        wbuf[k : k + 1, :] = jnp.exp(mmax[k : k + 1, :] - lt_a[dx, pl.ds(ys[dy], 1), :])

    def row_terms(k):
        return 10.0 * (obuf[k] * wbuf[k : k + 1, :] - lbuf[k].astype(F32))

    rw_x = []
    for k in range(G - 1, 0, -1):
        p = ORDER[k]
        rout[k] = row_terms(k).astype(BF16)
        cp = pltpu.make_async_remote_copy(
            rout.at[k], rin.at[k], rw_s.at[k], rw_r.at[k], device_id=plane(*p), device_id_type=MESH
        )
        cp.start()
        rw_x.append((cp, k))
    own_rt[...] = row_terms(0)

    for j, rows in enumerate(parts):
        acc = None
        for k, p in enumerate(ORDER):
            if j == 0:
                w_col = jnp.broadcast_to(wbuf[k : k + 1, :], (128, 256)).T
                for h in (slice(0, 128), slice(128, 256)):
                    us[k, :, h] = (gbuf[rel(*p), :, h].astype(F32) * w_col).astype(BF16)
            acc = add(acc, dot(ebuf[k, rows, :], us[k]))
        soft[rows, :] = acc

    core_send(1, soft)
    sums = functools.reduce(add, [stats_b[k, 4:8, :] for k in range(G)])
    coarse_all = sums[1:2, 0:1]
    loss_core[0] = jnp.broadcast_to(total(loss_rows) - sums[0:1, 0:1], (8, 128))
    lcp = pltpu.make_async_remote_copy(
        loss_core.at[0], loss_core.at[1], ls_s.at[0], ls_r.at[0], device_id=(other, g), device_id_type=MESH
    )
    lcp.start()
    core_merge(1, soft)
    lcp.wait_recv()
    loss_z[0] = loss_core[0] + loss_core[1]

    @functools.cache
    def lz_copy(d):
        return pltpu.make_async_remote_copy(
            loss_z.at[0], loss_z.at[d], ls_s.at[d], ls_r.at[d], device_id=column(d), device_id_type=MESH
        )

    for d in range(1, 8):
        lz_copy(d).start()

    for rows in parts:
        cpart[rows, :] = cpart_t[:, rows].T
    for d in range(1, 8):
        cgz_copy(d).wait_recv()

    cg_mine = cg_fin.at[c]
    cgc = pltpu.make_async_remote_copy(
        cg_mine, cg_mine, cgz_s.at[0], cgz_r.at[0], device_id=(other, g), device_id_type=MESH
    )
    cgc.start()
    z_merge(0)
    cgc.wait_recv()
    o_cg[...] = cg_fin[...].reshape(KC, D).astype(F32)
    z_merge(1)
    z_gathered(0)
    ca_copy(0).wait_recv()
    for j, rows in enumerate(parts):
        members = fin[0, j // 2, (j % 2) * 4 : (j % 2) * 4 + 4].reshape(256, D).astype(F32)
        p32 = protos[rows, :].astype(F32)
        norm = jnp.sqrt(jnp.sum(p32 * p32, axis=1, keepdims=True) + 1e-06)
        length = lax.rsqrt(jnp.sum(members * members, axis=1, keepdims=True) + 1e-06)
        o_new[rows, :] = 0.5 * p32 + (0.5 * norm) * (members * length)
        cpart[rows, :] = cpart[rows, :] - 2.5 * members

    z_gathered(1)

    half = (G - 1) // 2
    acc = own_rt[...]
    for cp, k in rw_x[:half]:
        cp.wait_recv()
        acc = acc + rin[k].astype(F32)
    own_rt[...] = acc
    for cp in gathers + lab_x + cgo_x + cga_x + sa_x + sb_x:
        cp.wait_send()
    for d in range(1, 8):
        cgz_copy(d).wait_send()
        for t in range(2):
            z_copy(t, d).wait_send()
    core_copy(0).wait_send()
    core_copy(1).wait_send()
    lcp.wait_send()
    for d in range(1, 8):
        za_copy(0, d).wait_send()
    cgc.wait_send()
    ca_copy(0).wait_send()

    for d in range(1, 8):
        lz_copy(d).wait_recv()
    fine = functools.reduce(add, [loss_z[d] for d in range(8)])
    o_loss[...] = fine[0:1, 0:1] * (1.0 / (G * G * ROWS)) + coarse_all * (1.0 / (KL * G))

    ca_copy(1).wait_recv()
    for j, rows in enumerate(parts):
        part = fin[1, j // 2, (j % 2) * 4 : (j % 2) * 4 + 4].reshape(256, D).astype(F32)
        o_pg[rows, :] = cpart[rows, :] + 2.5 * part
    for d in range(1, 8):
        lz_copy(d).wait_send()
        za_copy(1, d).wait_send()
    ca_copy(1).wait_send()

    acc = own_rt[...]
    for cp, k in rw_x[half:]:
        cp.wait_recv()
        acc = acc + rin[k].astype(F32)
    row_grad = acc.T
    unit = unit_s[...]
    inv = inv_s[:, 0:1]
    o_emb[...] = inv * (row_grad - unit * jnp.sum(unit * row_grad, axis=1, keepdims=True))
    for cp, _ in rw_x:
        cp.wait_send()


def body(embeddings, fine_labels, prototypes, coarse_protos, coarse_labels):
    vmem = pl.BlockSpec(memory_space=pltpu.VMEM)
    sem = pltpu.SemaphoreType.DMA
    scratch = [
        pltpu.VMEM((G, ROWS, D), BF16),
        pltpu.VMEM((G, 1, ROWS), jnp.int32),
        pltpu.VMEM((ROWS, D), F32),
        pltpu.VMEM((ROWS, 128), F32),
        pltpu.VMEM((D, KL), BF16),
        pltpu.VMEM((D, KC), BF16),
        pltpu.VMEM((KL, ROWS), F32),
        pltpu.VMEM((KL, ROWS), F32),
        pltpu.VMEM((G, KL, ROWS), BF16),
        pltpu.VMEM((G, D, ROWS), F32),
        pltpu.VMEM((G, D, ROWS), BF16),
        pltpu.VMEM((G, ROWS, D), BF16),
        pltpu.VMEM((G, D, ROWS), BF16),
        pltpu.VMEM((G, D, ROWS), BF16),
        pltpu.VMEM((D, ROWS), F32),
        pltpu.VMEM((KL, D), F32),
        pltpu.VMEM((KL, D), F32),
        pltpu.VMEM((KC, D), F32),
        pltpu.VMEM((D, KL), F32),
        pltpu.VMEM((KL, D), F32),
        pltpu.VMEM((G, 16, ROWS), F32),
        pltpu.VMEM((G, 8, ROWS), F32),
        pltpu.VMEM((G, ROWS), F32),
        pltpu.VMEM((4, 4, ROWS), F32),
        pltpu.VMEM((G, ROWS), F32),
        pltpu.VMEM((G, 8, 128), F32),
        pltpu.VMEM((G, 8, 128), F32),
        pltpu.VMEM((G, 8, 128), F32),
        pltpu.VMEM((2, 8, 64, D), BF16),
        pltpu.VMEM((2, 8, 64, D), BF16),
        pltpu.VMEM((2, 2, 8, 64, D), BF16),
        pltpu.VMEM((2, 8, 64, D), BF16),
        pltpu.VMEM((2, 2, 8, 64, D), BF16),
        pltpu.VMEM((2, 8, 128), F32),
        pltpu.VMEM((8, 8, 128), F32),
        sem((N_GATHER,)), sem((N_GATHER,)),
        sem((G,)), sem((G,)), sem((G,)), sem((G,)), sem((G,)), sem((G,)),
        sem((8,)), sem((8,)),
        sem((G,)), sem((G,)), sem((G,)), sem((G,)), sem((G,)), sem((G,)),
        sem((2,)), sem((2,)),
        sem((2, 8)), sem((2, 8)), sem((2, 8)), sem((2, 8)),
        sem((2,)), sem((2,)),
        sem((8,)), sem((8,)),
    ]
    outs = [
        pltpu.VMEM((ROWS, D), F32),
        pltpu.VMEM((KL, D), F32),
        pltpu.VMEM((KL, D), F32),
        pltpu.VMEM((KC, D), F32),
        jax.ShapeDtypeStruct((1, 1), F32),
    ]
    ge, gp, new, gc, loss = pl.pallas_call(
        kernel,
        out_shape=outs,
        in_specs=[vmem] * 5,
        out_specs=[vmem] * 5,
        scratch_shapes=scratch,
        compiler_params=pltpu.CompilerParams(
            collective_id=0, has_side_effects=True, vmem_limit_bytes=56 * 1024 * 1024
        ),
    )(embeddings, fine_labels.reshape(1, ROWS), prototypes, coarse_protos, coarse_labels.reshape(1, KC))
    return ge, gp, new, gc, loss.reshape(())


def solution(mesh):
    in_specs = (P(("rows", "group"), None), P(("rows", "group")), P("group", None), P(), P("group"))
    out_specs = (P(("rows", "group"), None), P("group", None), P("group", None), P(), P())
    return jax.shard_map(body, mesh=mesh, in_specs=in_specs, out_specs=out_specs, check_vma=False)
```

```python
import functools

import jax
import jax.numpy as jnp
from jax import lax
from jax.experimental import pallas as pl
from jax.experimental.pallas import tpu as pltpu
from jax.sharding import PartitionSpec as P

MESH = pl.DeviceIdType.MESH
F32 = jnp.float32
BF16 = jnp.bfloat16
ROWS = 256
D = 256
KL = 1024
KC = 1024
G = 16
NCH = KL // 256
N_GATHER = 40
NT = (((1,), (1,)), ((), ()))
LOG2E = 1.4426950408889634


def dot(a, b):
    return jnp.dot(a, b, preferred_element_type=F32)


def dot_nt(a, b):
    return lax.dot_general(a, b, NT, preferred_element_type=F32)


def column_sum(value):
    return jnp.sum(value, axis=0, keepdims=True)


def total(value):
    return jnp.sum(jnp.sum(value, axis=0, keepdims=True), axis=1, keepdims=True)


def rel(dx, dy):
    return (dx % 4) * 4 + dy % 4


ORDER = [(0, 0), (1, 0), (3, 0), (0, 1), (0, 3), (1, 1), (1, 3), (3, 1), (3, 3), (0, 2), (1, 2), (3, 2)]
ORDER += [(2, 0), (2, 1), (2, 3), (2, 2)]
PEERS = ORDER[1:]
ROW_ORDER = [(2, 2), (2, 1), (1, 2), (2, 3), (3, 2), (2, 0), (0, 2), (1, 1), (3, 3), (1, 3), (3, 1)]
ROW_ORDER += [(1, 0), (0, 1), (3, 0), (0, 3)]
SLOT = {0: 0, 1: 1, 3: 2}


def kernel(
    emb, lab, protos, coarse, clab,
    o_emb, o_pg, o_new, o_cg, o_loss,
    gbuf, labs, unit_s, inv_s, protos_t, coarse_t, lscr, lscr2, ebuf, obuf, lbuf, us, rout, rin, own_rt,
    mem, soft, cg, cpart_t, cpart, stats_a, stats_b, mmax, lt_a, wbuf,
    cg_x, cg_y, cg_fin, core_in, z_out, z_in, fin, loss_core, loss_z,
    gs, gr, labs_s, labs_r, cgx_s, cgx_r, cgy_s, cgy_r, cga_s, cga_r, cgz_s, cgz_r, sa_s, sa_r, sb_s, sb_r,
    rw_s, rw_r, co_s, co_r, zo_s, zo_r, za_s, za_r, ca_s, ca_r, ls_s, ls_r,
):
    r = lax.axis_index("rows")
    g = lax.axis_index("group")
    z, c = r // 2, lax.rem(r, 2)
    x, y = g // 4, lax.rem(g, 4)
    other = r + 1 - 2 * c
    xs = [lax.rem(x + i, 4) * 4 for i in range(4)]
    ys = [lax.rem(y + i, 4) for i in range(4)]

    def plane(dx, dy):
        return (r, xs[dx % 4] + ys[dy % 4])

    def column(d):
        return (lax.rem(r + 2 * d, 16), g)

    def zof(d):
        return lax.rem(z + d, 8)

    barrier = pltpu.get_barrier_semaphore()
    for d in range(1, 8):
        pl.semaphore_signal(barrier, inc=1, device_id=column(d), device_id_type=MESH)
    for p in PEERS:
        pl.semaphore_signal(barrier, inc=1, device_id=plane(*p), device_id_type=MESH)
    pl.semaphore_signal(barrier, inc=1, device_id=(other, g), device_id_type=MESH)

    e32 = emb[...].astype(F32)
    inv = lax.rsqrt(jnp.sum(e32 * e32, axis=1, keepdims=True) + 1e-06)
    unit = e32 * inv
    unit_s[...] = unit
    inv_s[...] = jnp.broadcast_to(inv, (ROWS, 128))
    gbuf[0] = unit.astype(BF16)
    labs[0] = lab[...]

    pl.semaphore_wait(barrier, 23)

    A, B = (0, 128), (128, 128)
    A0, A1, B0, B1 = (0, 64), (64, 64), (128, 64), (192, 64)
    gathers = []

    def send(bx, by, rows, dx, dy):
        k = len(gathers)
        cp = pltpu.make_async_remote_copy(
            gbuf.at[rel(bx, by), pl.ds(*rows)], gbuf.at[rel(bx - dx, by - dy), pl.ds(*rows)],
            gs.at[k], gr.at[k], device_id=plane(dx, dy), device_id_type=MESH,
        )
        cp.start()
        gathers.append(cp)
        return cp

    def both_y(bx, by):
        return send(bx, by, A, 0, 1), send(bx, by, A, 0, 3)

    def both_x(bx, by):
        return send(bx, by, B, 1, 0), send(bx, by, B, 3, 0)

    def on_y(cp, bx, up):
        cp.wait_recv()
        return send(bx, 3, A0, 0, 1) if up else send(bx, 1, A1, 0, 3)

    def on_x(cp, by, up):
        cp.wait_recv()
        return send(3, by, B0, 1, 0) if up else send(1, by, B1, 3, 0)

    def arrived(*copies):
        for cp in copies:
            cp.wait_recv()

    def exchange(src, dst, send_sem, recv_sem):
        copies = []
        for k, p in enumerate(PEERS):
            cp = pltpu.make_async_remote_copy(
                src(k), dst(rel(-p[0], -p[1])), send_sem.at[k], recv_sem.at[k],
                device_id=plane(*p), device_id_type=MESH,
            )
            cp.start()
            copies.append(cp)
        return copies

    a1, a2 = send(0, 0, A, 1, 0), send(0, 0, A, 3, 0)
    b1, b2 = send(0, 0, B, 0, 1), send(0, 0, B, 0, 3)
    a3, a4 = both_y(0, 0)
    b3, b4 = both_x(0, 0)
    lab_x = exchange(lambda k: labs.at[0], lambda s: labs.at[s], labs_s, labs_r)

    iota = lax.broadcasted_iota(jnp.int32, (256, 256), 0)
    iota_half = iota.astype(F32).astype(BF16)
    parts = [slice(j * 256, (j + 1) * 256) for j in range(NCH)]

    for rows in parts:
        protos_t[:, rows] = protos[rows, :].astype(F32).T.astype(BF16)
        coarse_t[:, rows] = coarse[rows, :].astype(F32).T.astype(BF16)

    def logits_peak(left, u):
        peak = None
        for rows in parts:
            logits = dot_nt(left[rows, :], u)
            lscr[rows, :] = logits
            peak = logits if peak is None else jnp.maximum(peak, logits)
        return jnp.max(peak, axis=0, keepdims=True)

    def add(a, b):
        return b if a is None else a + b

    def onehot(labels, j):
        near = labels - j * 256
        near = jnp.where((near >= 0) & (near < 256), near, -1).astype(F32).astype(BF16)
        return jnp.where(iota_half == near, jnp.ones((), BF16), jnp.zeros((), BF16))

    def coarse_block(kb):
        u = protos[parts[kb], :]
        labels = clab[:, parts[kb]]
        peak = logits_peak(coarse, u)
        expsum = target = out = None
        for j, rows in enumerate(parts):
            logits = lscr[rows, :]
            target = add(target, jnp.where(iota == labels - j * 256, logits, 0.0))
            e = jnp.exp2((logits - peak) * (10.0 * LOG2E))
            expsum = add(expsum, e)
            lscr2[rows, :] = e
        expsum = column_sum(expsum)
        share = 10.0 / expsum
        for j, rows in enumerate(parts):
            delta = (lscr2[rows, :] * share - jnp.where(iota == labels - j * 256, 10.0, 0.0)).astype(BF16)
            out = add(out, dot(coarse_t[:, rows], delta))
            if kb == 0:
                cg[rows, :] = dot(delta, u)
            else:
                cg[rows, :] += dot(delta, u)
        cpart_t[:, parts[kb]] = out
        return total(10.0 * (peak - column_sum(target)) + jnp.log(expsum))

    def local_labels(p):
        return labs[rel(*p)] - g * KL

    def first_pass(k, prev):
        dx, dy = ORDER[k]
        u = gbuf[rel(dx, dy)]
        peak = logits_peak(protos, u)
        labels = local_labels(ORDER[k])
        expsum = out = None
        for j, rows in enumerate(parts):
            e = jnp.exp2((lscr[rows, :] - peak) * (10.0 * LOG2E))
            expsum = add(expsum, e)
            ebuf[k, rows, :] = e.astype(BF16)
            if prev is not None:
                out = add(out, dot(protos_t[:, rows], ebuf[prev, rows, :]))
            member = dot(onehot(labels, j), u)
            if k == 0:
                mem[rows, :] = member
            else:
                mem[rows, :] += member
        if prev is not None:
            obuf[prev] = out
        mmax[k : k + 1, :] = 10.0 * peak
        lse = 10.0 * peak + jnp.log(column_sum(expsum))
        if dx == 2:
            stats_b[0, pl.ds(ys[dy], 1), :] = lse
        else:
            stats_a[0, pl.ds(SLOT[dx] * 4 + ys[dy], 1), :] = lse

    def label_rows(*which):
        for k in which:
            labels = local_labels(ORDER[k])
            out = None
            for j, rows in enumerate(parts):
                out = add(out, dot(protos_t[:, rows], onehot(labels, j)))
            lbuf[k] = out.astype(BF16)

    coarse_loss = coarse_block(0)
    first_pass(0, None)

    a1.wait_recv()
    f1 = send(3, 0, A0, 1, 0)
    p1, p2 = both_y(3, 0)
    b1.wait_recv()
    g1 = send(0, 3, B0, 0, 1)
    q1, q2 = both_x(0, 3)
    a2.wait_recv()
    f2 = send(1, 0, A1, 3, 0)
    p3, p4 = both_y(1, 0)
    b2.wait_recv()
    g2 = send(0, 1, B1, 0, 3)
    q3, q4 = both_x(0, 1)
    coarse_loss = coarse_loss + coarse_block(1)
    a3f, b3f, a4f, b4f = on_y(a3, 0, True), on_x(b3, 0, True), on_y(a4, 0, False), on_x(b4, 0, False)
    coarse_loss = coarse_loss + coarse_block(2)
    coarse_loss = coarse_loss + coarse_block(3)

    base = c * 512 + z * 64

    def slice_of(at):
        return cg.at[pl.ds(pl.multiple_of(base + 16 * at, 16), 16), :]

    def line_copies(src, dst, send_sem, recv_sem, target):
        copies = []
        for d in (2, 1, 3):
            cp = pltpu.make_async_remote_copy(
                src(d), dst, send_sem.at[d], recv_sem.at[d], device_id=target(d), device_id_type=MESH
            )
            cp.start()
            copies.append(cp)
        return copies

    cgx_c = line_copies(lambda d: slice_of(lax.rem(x + d, 4)), cg_x.at[x], cgx_s, cgx_r, lambda d: plane(d, 0))
    cg_x[x] = slice_of(x)[...]

    arrived(*lab_x)
    arrived(f1, f2)
    p5, p6 = both_y(2, 0)
    arrived(g1, g2)
    q5, q6 = both_x(0, 2)
    first_pass(1, 0)
    first_pass(2, 1)
    p1f, q1f, p2f, q2f = on_y(p1, 3, True), on_x(q1, 3, True), on_y(p2, 3, False), on_x(q2, 3, False)
    first_pass(3, 2)
    p3f, q3f, p4f, q4f = on_y(p3, 1, True), on_x(q3, 1, True), on_y(p4, 1, False), on_x(q4, 1, False)
    first_pass(4, 3)
    first_pass(5, 4)
    p5f, q5f, p6f, q6f = on_y(p5, 2, True), on_x(q5, 2, True), on_y(p6, 2, False), on_x(q6, 2, False)
    first_pass(6, 5)
    arrived(*cgx_c)
    cg_y[y] = cg_x[0] + cg_x[1] + cg_x[2] + cg_x[3]
    cgy_c = line_copies(lambda d: cg_y.at[y], cg_y.at[y], cgy_s, cgy_r, lambda d: plane(0, d))
    first_pass(7, 6)
    first_pass(8, 7)
    label_rows(0, 1, 2)
    arrived(a3f, b3f, a4f, b4f)
    first_pass(9, 8)
    arrived(p1f, p2f, p3f, p4f)
    first_pass(10, 9)
    arrived(*cgy_c)
    tile = (KC / (KL * G)) * (cg_y[0] + cg_y[1] + cg_y[2] + cg_y[3])
    own_rows = pl.ds(pl.multiple_of(16 * x, 16), 16)
    cg_fin[c, z, own_rows, :] = tile.astype(BF16)
    cg_part = cg_fin.at[c, z, own_rows]
    cga_c = line_copies(lambda d: cg_part, cg_part, cga_s, cga_r, lambda d: plane(d, 0))
    first_pass(11, 10)
    sa_x = exchange(lambda k: stats_a.at[0], lambda s: stats_a.at[s], sa_s, sa_r)
    first_pass(12, 11)
    label_rows(3, 4, 5)
    arrived(q1f, q2f, q3f, q4f)
    first_pass(13, 12)
    first_pass(14, 13)

    arrived(*cga_c)

    @functools.cache
    def cgz_copy(d):
        slot = cg_fin.at[c, z]
        return pltpu.make_async_remote_copy(
            slot, slot, cgz_s.at[d], cgz_r.at[d], device_id=column(d), device_id_type=MESH
        )

    for d in range(1, 8):
        cgz_copy(d).start()

    label_rows(6, 7, 8, 9)
    arrived(p5f, q5f, p6f, q6f)
    first_pass(15, 14)
    target = 10.0 * total(mem[...] * protos[...].astype(F32))
    head = lax.broadcasted_iota(jnp.int32, (4, ROWS), 0) == 0
    stats_b[0, 4:8, :] = jnp.where(head, target, coarse_loss)
    sb_x = exchange(lambda k: stats_b.at[0], lambda s: stats_b.at[s], sb_s, sb_r)

    @functools.cache
    def core_copy(t):
        return pltpu.make_async_remote_copy(
            z_out.at[t, 1 - c], core_in.at[t], co_s.at[t], co_r.at[t], device_id=(other, g), device_id_type=MESH
        )

    @functools.cache
    def z_copy(t, d):
        return pltpu.make_async_remote_copy(
            z_out.at[t, c, zof(d)], z_in.at[t, d], zo_s.at[t, d], zo_r.at[t, d],
            device_id=column(d), device_id_type=MESH,
        )

    @functools.cache
    def za_copy(t, d):
        slot = fin.at[t, c, z]
        return pltpu.make_async_remote_copy(
            slot, slot, za_s.at[t, d], za_r.at[t, d], device_id=column(d), device_id_type=MESH
        )

    @functools.cache
    def ca_copy(t):
        slot = fin.at[t, c]
        return pltpu.make_async_remote_copy(
            slot, slot, ca_s.at[t], ca_r.at[t], device_id=(other, g), device_id_type=MESH
        )

    def core_send(t, src):
        half = src[pl.ds(pl.multiple_of((1 - c) * 512, 512), 512), :].astype(BF16)
        z_out[t, 1 - c] = half.reshape(8, 64, D)
        core_copy(t).start()

    def core_merge(t, src):
        core_copy(t).wait_recv()
        half = src[pl.ds(pl.multiple_of(c * 512, 512), 512), :].reshape(8, 64, D)
        z_out[t, c] = (half + core_in[t].astype(F32)).astype(BF16)

        for d in range(1, 8):
            z_copy(t, d).start()

    def z_merge(t):
        for d in range(1, 8):
            z_copy(t, d).wait_recv()

        acc = z_out[t, c, z].astype(F32)
        for d in range(1, 8):
            acc = acc + z_in[t, d].astype(F32)
        fin[t, c, z] = acc.astype(BF16)

        for d in range(1, 8):
            za_copy(t, d).start()

    def z_gathered(t):
        for d in range(1, 8):
            za_copy(t, d).wait_recv()

        ca_copy(t).start()

    core_send(0, mem)

    last = None
    for rows in parts:
        last = add(last, dot(protos_t[:, rows], ebuf[15, rows, :]))
    obuf[15] = last
    label_rows(10, 11, 12, 13, 14, 15)
    core_merge(0, mem)

    arrived(*sa_x)
    arrived(*sb_x)

    def line(a, b, dx):
        away = (dx - a) % 4
        if away == 2:
            return stats_b[rel(a, b), 0:4, :]
        return stats_a[rel(a, b), SLOT[away] * 4 : SLOT[away] * 4 + 4, :]

    loss_rows = None
    for dx in range(4):
        lines = [line(a, b, dx) for a in range(4) for b in range(4)]
        peak = functools.reduce(jnp.maximum, lines)
        log_total = peak + jnp.log(functools.reduce(add, [jnp.exp(v - peak) for v in lines]))
        lt_a[dx] = log_total
        loss_rows = add(loss_rows, log_total)
    for k, (dx, dy) in enumerate(ORDER):
        wbuf[k : k + 1, :] = jnp.exp(mmax[k : k + 1, :] - lt_a[dx, pl.ds(ys[dy], 1), :])

    def row_terms(k):
        return 10.0 * (obuf[k] * wbuf[k : k + 1, :] - lbuf[k].astype(F32))

    rw_x = []
    for p in ROW_ORDER:
        k = ORDER.index(p)
        rout[k] = row_terms(k).astype(BF16)
        cp = pltpu.make_async_remote_copy(
            rout.at[k], rin.at[k], rw_s.at[k], rw_r.at[k], device_id=plane(*p), device_id_type=MESH
        )
        cp.start()
        rw_x.append((cp, k))
    for j, rows in enumerate(parts):
        acc = None
        for k, p in enumerate(ORDER):
            if j == 0:
                w_col = jnp.broadcast_to(wbuf[k : k + 1, :], (128, 256)).T
                for h in (slice(0, 128), slice(128, 256)):
                    us[k, :, h] = (gbuf[rel(*p), :, h].astype(F32) * w_col).astype(BF16)
            acc = add(acc, dot(ebuf[k, rows, :], us[k]))
        soft[rows, :] = acc

    core_send(1, soft)
    own_rt[...] = row_terms(0)
    sums = functools.reduce(add, [stats_b[k, 4:8, :] for k in range(G)])
    coarse_all = sums[1:2, 0:1]
    loss_core[0] = jnp.broadcast_to(total(loss_rows) - sums[0:1, 0:1], (8, 128))
    lcp = pltpu.make_async_remote_copy(
        loss_core.at[0], loss_core.at[1], ls_s.at[0], ls_r.at[0], device_id=(other, g), device_id_type=MESH
    )
    lcp.start()
    core_merge(1, soft)
    lcp.wait_recv()
    loss_z[0] = loss_core[0] + loss_core[1]

    @functools.cache
    def lz_copy(d):
        return pltpu.make_async_remote_copy(
            loss_z.at[0], loss_z.at[d], ls_s.at[d], ls_r.at[d], device_id=column(d), device_id_type=MESH
        )

    for d in range(1, 8):
        lz_copy(d).start()

    for rows in parts:
        cpart[rows, :] = cpart_t[:, rows].T
    for d in range(1, 8):
        cgz_copy(d).wait_recv()

    cg_mine = cg_fin.at[c]
    cgc = pltpu.make_async_remote_copy(
        cg_mine, cg_mine, cgz_s.at[0], cgz_r.at[0], device_id=(other, g), device_id_type=MESH
    )
    cgc.start()
    z_merge(0)
    cgc.wait_recv()
    o_cg[...] = cg_fin[...].reshape(KC, D).astype(F32)
    z_merge(1)
    z_gathered(0)
    ca_copy(0).wait_recv()
    for j, rows in enumerate(parts):
        members = fin[0, j // 2, (j % 2) * 4 : (j % 2) * 4 + 4].reshape(256, D).astype(F32)
        p32 = protos[rows, :].astype(F32)
        norm = jnp.sqrt(jnp.sum(p32 * p32, axis=1, keepdims=True) + 1e-06)
        length = lax.rsqrt(jnp.sum(members * members, axis=1, keepdims=True) + 1e-06)
        o_new[rows, :] = 0.5 * p32 + (0.5 * norm) * (members * length)
        cpart[rows, :] = cpart[rows, :] - 2.5 * members

    z_gathered(1)

    half = (G - 1) // 2
    acc = own_rt[...]
    for cp, k in rw_x[:half]:
        cp.wait_recv()
        acc = acc + rin[k].astype(F32)
    own_rt[...] = acc
    for cp in gathers + lab_x + cgx_c + cgy_c + cga_c + sa_x + sb_x:
        cp.wait_send()
    for d in range(1, 8):
        cgz_copy(d).wait_send()
        for t in range(2):
            z_copy(t, d).wait_send()
    core_copy(0).wait_send()
    core_copy(1).wait_send()
    lcp.wait_send()
    for d in range(1, 8):
        za_copy(0, d).wait_send()
    cgc.wait_send()
    ca_copy(0).wait_send()

    for d in range(1, 8):
        lz_copy(d).wait_recv()
    fine = functools.reduce(add, [loss_z[d] for d in range(8)])
    o_loss[...] = fine[0:1, 0:1] * (1.0 / (G * G * ROWS)) + coarse_all * (1.0 / (KL * G))

    ca_copy(1).wait_recv()
    for j, rows in enumerate(parts):
        part = fin[1, j // 2, (j % 2) * 4 : (j % 2) * 4 + 4].reshape(256, D).astype(F32)
        o_pg[rows, :] = cpart[rows, :] + 2.5 * part
    for d in range(1, 8):
        lz_copy(d).wait_send()
        za_copy(1, d).wait_send()
    ca_copy(1).wait_send()

    acc = own_rt[...]
    for cp, k in rw_x[half:]:
        cp.wait_recv()
        acc = acc + rin[k].astype(F32)
    row_grad = acc.T
    unit = unit_s[...]
    inv = inv_s[:, 0:1]
    o_emb[...] = inv * (row_grad - unit * jnp.sum(unit * row_grad, axis=1, keepdims=True))
    for cp, _ in rw_x:
        cp.wait_send()


def body(embeddings, fine_labels, prototypes, coarse_protos, coarse_labels):
    vmem = pl.BlockSpec(memory_space=pltpu.VMEM)
    sem = pltpu.SemaphoreType.DMA
    scratch = [
        pltpu.VMEM((G, ROWS, D), BF16),
        pltpu.VMEM((G, 1, ROWS), jnp.int32),
        pltpu.VMEM((ROWS, D), F32),
        pltpu.VMEM((ROWS, 128), F32),
        pltpu.VMEM((D, KL), BF16),
        pltpu.VMEM((D, KC), BF16),
        pltpu.VMEM((KL, ROWS), F32),
        pltpu.VMEM((KL, ROWS), F32),
        pltpu.VMEM((G, KL, ROWS), BF16),
        pltpu.VMEM((G, D, ROWS), F32),
        pltpu.VMEM((G, D, ROWS), BF16),
        pltpu.VMEM((G, ROWS, D), BF16),
        pltpu.VMEM((G, D, ROWS), BF16),
        pltpu.VMEM((G, D, ROWS), BF16),
        pltpu.VMEM((D, ROWS), F32),
        pltpu.VMEM((KL, D), F32),
        pltpu.VMEM((KL, D), F32),
        pltpu.VMEM((KC, D), F32),
        pltpu.VMEM((D, KL), F32),
        pltpu.VMEM((KL, D), F32),
        pltpu.VMEM((G, 16, ROWS), F32),
        pltpu.VMEM((G, 8, ROWS), F32),
        pltpu.VMEM((G, ROWS), F32),
        pltpu.VMEM((4, 4, ROWS), F32),
        pltpu.VMEM((G, ROWS), F32),
        pltpu.VMEM((4, 16, D), F32),
        pltpu.VMEM((4, 16, D), F32),
        pltpu.VMEM((2, 8, 64, D), BF16),
        pltpu.VMEM((2, 8, 64, D), BF16),
        pltpu.VMEM((2, 2, 8, 64, D), BF16),
        pltpu.VMEM((2, 8, 64, D), BF16),
        pltpu.VMEM((2, 2, 8, 64, D), BF16),
        pltpu.VMEM((2, 8, 128), F32),
        pltpu.VMEM((8, 8, 128), F32),
        sem((N_GATHER,)), sem((N_GATHER,)),
        sem((G,)), sem((G,)), sem((4,)), sem((4,)), sem((4,)), sem((4,)), sem((4,)), sem((4,)),
        sem((8,)), sem((8,)),
        sem((G,)), sem((G,)), sem((G,)), sem((G,)), sem((G,)), sem((G,)),
        sem((2,)), sem((2,)),
        sem((2, 8)), sem((2, 8)), sem((2, 8)), sem((2, 8)),
        sem((2,)), sem((2,)),
        sem((8,)), sem((8,)),
    ]
    outs = [
        pltpu.VMEM((ROWS, D), F32),
        pltpu.VMEM((KL, D), F32),
        pltpu.VMEM((KL, D), F32),
        pltpu.VMEM((KC, D), F32),
        jax.ShapeDtypeStruct((1, 1), F32),
    ]
    ge, gp, new, gc, loss = pl.pallas_call(
        kernel,
        out_shape=outs,
        in_specs=[vmem] * 5,
        out_specs=[vmem] * 5,
        scratch_shapes=scratch,
        compiler_params=pltpu.CompilerParams(
            collective_id=0, has_side_effects=True, vmem_limit_bytes=56 * 1024 * 1024
        ),
    )(embeddings, fine_labels.reshape(1, ROWS), prototypes, coarse_protos, coarse_labels.reshape(1, KC))
    return ge, gp, new, gc, loss.reshape(())


def solution(mesh):
    in_specs = (P(("rows", "group"), None), P(("rows", "group")), P("group", None), P(), P("group"))
    out_specs = (P(("rows", "group"), None), P("group", None), P("group", None), P(), P())
    return jax.shard_map(body, mesh=mesh, in_specs=in_specs, out_specs=out_specs, check_vma=False)
```

```python
import functools

import jax
import jax.numpy as jnp
from jax import lax
from jax.experimental import pallas as pl
from jax.experimental.pallas import tpu as pltpu
from jax.sharding import PartitionSpec as P

MESH = pl.DeviceIdType.MESH
F32 = jnp.float32
BF16 = jnp.bfloat16
ROWS = 256
D = 256
KL = 1024
KC = 1024
G = 16
NCH = KL // 256
N_GATHER = 40
NT = (((1,), (1,)), ((), ()))
LOG2E = 1.4426950408889634


def dot(a, b):
    return jnp.dot(a, b, preferred_element_type=F32)


def dot_nt(a, b):
    return lax.dot_general(a, b, NT, preferred_element_type=F32)


def column_sum(value):
    return jnp.sum(value, axis=0, keepdims=True)


def total(value):
    return jnp.sum(jnp.sum(value, axis=0, keepdims=True), axis=1, keepdims=True)


def rel(dx, dy):
    return (dx % 4) * 4 + dy % 4


ORDER = [(0, 0), (1, 0), (3, 0), (0, 1), (0, 3), (1, 1), (1, 3), (3, 1), (3, 3), (0, 2), (1, 2), (3, 2)]
ORDER += [(2, 0), (2, 1), (2, 3), (2, 2)]
PEERS = ORDER[1:]
ROW_ORDER = [(2, 2), (2, 1), (1, 2), (2, 3), (3, 2), (2, 0), (0, 2), (1, 1), (3, 3), (1, 3), (3, 1)]
ROW_ORDER += [(1, 0), (0, 1), (3, 0), (0, 3)]
SLOT = {0: 0, 1: 1, 3: 2}


def kernel(
    emb, lab, protos, coarse, clab,
    o_emb, o_pg, o_new, o_cg, o_loss,
    gbuf, labs, unit_s, inv_s, protos_t, coarse_t, lscr, lscr2, ebuf, obuf, lbuf, us, rout, rin, own_rt,
    mem, soft, cg, cpart_t, cpart, stats_a, stats_b, mmax, lt_a, wbuf,
    cg_x, cg_y, cg_fin, core_in, z_out, z_in, fin, loss_core, loss_z,
    gs, gr, labs_s, labs_r, cgx_s, cgx_r, cgy_s, cgy_r, cga_s, cga_r, cgz_s, cgz_r, sa_s, sa_r, sb_s, sb_r,
    rw_s, rw_r, co_s, co_r, zo_s, zo_r, za_s, za_r, ca_s, ca_r, ls_s, ls_r,
):
    r = lax.axis_index("rows")
    g = lax.axis_index("group")
    z, c = r // 2, lax.rem(r, 2)
    x, y = g // 4, lax.rem(g, 4)
    other = r + 1 - 2 * c
    xs = [lax.rem(x + i, 4) * 4 for i in range(4)]
    ys = [lax.rem(y + i, 4) for i in range(4)]

    def plane(dx, dy):
        return (r, xs[dx % 4] + ys[dy % 4])

    def column(d):
        return (lax.rem(r + 2 * d, 16), g)

    def zof(d):
        return lax.rem(z + d, 8)

    barrier = pltpu.get_barrier_semaphore()
    for d in range(1, 8):
        pl.semaphore_signal(barrier, inc=1, device_id=column(d), device_id_type=MESH)
    for p in PEERS:
        pl.semaphore_signal(barrier, inc=1, device_id=plane(*p), device_id_type=MESH)
    pl.semaphore_signal(barrier, inc=1, device_id=(other, g), device_id_type=MESH)

    e32 = emb[...].astype(F32)
    inv = lax.rsqrt(jnp.sum(e32 * e32, axis=1, keepdims=True) + 1e-06)
    unit = e32 * inv
    unit_s[...] = unit
    inv_s[...] = jnp.broadcast_to(inv, (ROWS, 128))
    gbuf[0] = unit.astype(BF16)
    labs[0] = lab[...]

    pl.semaphore_wait(barrier, 23)

    A, B = (0, 128), (128, 128)
    A0, A1, B0, B1 = (0, 64), (64, 64), (128, 64), (192, 64)
    gathers = []

    def send(bx, by, rows, dx, dy):
        k = len(gathers)
        cp = pltpu.make_async_remote_copy(
            gbuf.at[rel(bx, by), pl.ds(*rows)], gbuf.at[rel(bx - dx, by - dy), pl.ds(*rows)],
            gs.at[k], gr.at[k], device_id=plane(dx, dy), device_id_type=MESH,
        )
        cp.start()
        gathers.append(cp)
        return cp

    def both_y(bx, by):
        return send(bx, by, A, 0, 1), send(bx, by, A, 0, 3)

    def both_x(bx, by):
        return send(bx, by, B, 1, 0), send(bx, by, B, 3, 0)

    def on_y(cp, bx, up):
        cp.wait_recv()
        return send(bx, 3, A0, 0, 1) if up else send(bx, 1, A1, 0, 3)

    def on_x(cp, by, up):
        cp.wait_recv()
        return send(3, by, B0, 1, 0) if up else send(1, by, B1, 3, 0)

    def arrived(*copies):
        for cp in copies:
            cp.wait_recv()

    def exchange(src, dst, send_sem, recv_sem):
        copies = []
        for k, p in enumerate(PEERS):
            cp = pltpu.make_async_remote_copy(
                src(k), dst(rel(-p[0], -p[1])), send_sem.at[k], recv_sem.at[k],
                device_id=plane(*p), device_id_type=MESH,
            )
            cp.start()
            copies.append(cp)
        return copies

    a1, a2 = send(0, 0, A, 1, 0), send(0, 0, A, 3, 0)
    b1, b2 = send(0, 0, B, 0, 1), send(0, 0, B, 0, 3)
    a3, a4 = both_y(0, 0)
    b3, b4 = both_x(0, 0)
    lab_x = exchange(lambda k: labs.at[0], lambda s: labs.at[s], labs_s, labs_r)

    iota = lax.broadcasted_iota(jnp.int32, (256, 256), 0)
    iota_half = iota.astype(F32).astype(BF16)
    parts = [slice(j * 256, (j + 1) * 256) for j in range(NCH)]

    for rows in parts:
        protos_t[:, rows] = protos[rows, :].astype(F32).T.astype(BF16)
        coarse_t[:, rows] = coarse[rows, :].astype(F32).T.astype(BF16)

    def logits_peak(left, u):
        peak = None
        for rows in parts:
            logits = dot_nt(left[rows, :], u)
            lscr[rows, :] = logits
            peak = logits if peak is None else jnp.maximum(peak, logits)
        return jnp.max(peak, axis=0, keepdims=True)

    def add(a, b):
        return b if a is None else a + b

    def onehot(labels, j):
        near = labels - j * 256
        near = jnp.where((near >= 0) & (near < 256), near, -1).astype(F32).astype(BF16)
        return jnp.where(iota_half == near, jnp.ones((), BF16), jnp.zeros((), BF16))

    def coarse_block(kb):
        u = protos[parts[kb], :]
        labels = clab[:, parts[kb]]
        peak = logits_peak(coarse, u)
        expsum = target = out = None
        for j, rows in enumerate(parts):
            logits = lscr[rows, :]
            target = add(target, jnp.where(iota == labels - j * 256, logits, 0.0))
            e = jnp.exp2((logits - peak) * (10.0 * LOG2E))
            expsum = add(expsum, e)
            lscr2[rows, :] = e
        expsum = column_sum(expsum)
        share = 10.0 / expsum
        for j, rows in enumerate(parts):
            delta = (lscr2[rows, :] * share - jnp.where(iota == labels - j * 256, 10.0, 0.0)).astype(BF16)
            out = add(out, dot(coarse_t[:, rows], delta))
            if kb == 0:
                cg[rows, :] = dot(delta, u)
            else:
                cg[rows, :] += dot(delta, u)
        cpart_t[:, parts[kb]] = out
        return total(10.0 * (peak - column_sum(target)) + jnp.log(expsum))

    def local_labels(p):
        return labs[rel(*p)] - g * KL

    def first_pass(k, prev):
        dx, dy = ORDER[k]
        u = gbuf[rel(dx, dy)]
        peak = logits_peak(protos, u)
        labels = local_labels(ORDER[k])
        expsum = out = None
        for j, rows in enumerate(parts):
            e = jnp.exp2((lscr[rows, :] - peak) * (10.0 * LOG2E))
            expsum = add(expsum, e)
            ebuf[k, rows, :] = e.astype(BF16)
            if prev is not None:
                out = add(out, dot(protos_t[:, rows], ebuf[prev, rows, :]))
            member = dot(onehot(labels, j), u)
            if k == 0:
                mem[rows, :] = member
            else:
                mem[rows, :] += member
        if prev is not None:
            obuf[prev] = out
        mmax[k : k + 1, :] = 10.0 * peak
        lse = 10.0 * peak + jnp.log(column_sum(expsum))
        if dx == 2:
            stats_b[0, pl.ds(ys[dy], 1), :] = lse
        else:
            stats_a[0, pl.ds(SLOT[dx] * 4 + ys[dy], 1), :] = lse

    def label_rows(*which):
        for k in which:
            labels = local_labels(ORDER[k])
            out = None
            for j, rows in enumerate(parts):
                out = add(out, dot(protos_t[:, rows], onehot(labels, j)))
            lbuf[k] = out.astype(BF16)

    coarse_loss = coarse_block(0)
    first_pass(0, None)

    a1.wait_recv()
    f1 = send(3, 0, A0, 1, 0)
    p1, p2 = both_y(3, 0)
    b1.wait_recv()
    g1 = send(0, 3, B0, 0, 1)
    q1, q2 = both_x(0, 3)
    a2.wait_recv()
    f2 = send(1, 0, A1, 3, 0)
    p3, p4 = both_y(1, 0)
    b2.wait_recv()
    g2 = send(0, 1, B1, 0, 3)
    q3, q4 = both_x(0, 1)
    coarse_loss = coarse_loss + coarse_block(1)
    a3f, b3f, a4f, b4f = on_y(a3, 0, True), on_x(b3, 0, True), on_y(a4, 0, False), on_x(b4, 0, False)
    coarse_loss = coarse_loss + coarse_block(2)
    arrived(f1, f2)
    p5, p6 = both_y(2, 0)
    arrived(g1, g2)
    q5, q6 = both_x(0, 2)
    coarse_loss = coarse_loss + coarse_block(3)

    base = c * 512 + z * 64

    def slice_of(at):
        return cg.at[pl.ds(pl.multiple_of(base + 16 * at, 16), 16), :]

    def line_copies(src, dst, send_sem, recv_sem, target):
        copies = []
        for d in (2, 1, 3):
            cp = pltpu.make_async_remote_copy(
                src(d), dst, send_sem.at[d], recv_sem.at[d], device_id=target(d), device_id_type=MESH
            )
            cp.start()
            copies.append(cp)
        return copies

    cgx_c = line_copies(lambda d: slice_of(lax.rem(x + d, 4)), cg_x.at[x], cgx_s, cgx_r, lambda d: plane(d, 0))
    cg_x[x] = slice_of(x)[...]

    arrived(*lab_x)
    first_pass(1, 0)
    p1f, q1f, p2f, q2f = on_y(p1, 3, True), on_x(q1, 3, True), on_y(p2, 3, False), on_x(q2, 3, False)
    first_pass(2, 1)
    p3f, q3f, p4f, q4f = on_y(p3, 1, True), on_x(q3, 1, True), on_y(p4, 1, False), on_x(q4, 1, False)
    first_pass(3, 2)
    first_pass(4, 3)
    p5f, q5f, p6f, q6f = on_y(p5, 2, True), on_x(q5, 2, True), on_y(p6, 2, False), on_x(q6, 2, False)
    first_pass(5, 4)
    first_pass(6, 5)
    arrived(*cgx_c)
    cg_y[y] = cg_x[0] + cg_x[1] + cg_x[2] + cg_x[3]
    cgy_c = line_copies(lambda d: cg_y.at[y], cg_y.at[y], cgy_s, cgy_r, lambda d: plane(0, d))
    first_pass(7, 6)
    first_pass(8, 7)
    label_rows(0, 1, 2)
    arrived(a3f, b3f, a4f, b4f)
    first_pass(9, 8)
    arrived(p1f, p2f, p3f, p4f)
    first_pass(10, 9)
    arrived(*cgy_c)
    tile = (KC / (KL * G)) * (cg_y[0] + cg_y[1] + cg_y[2] + cg_y[3])
    own_rows = pl.ds(pl.multiple_of(16 * x, 16), 16)
    cg_fin[c, z, own_rows, :] = tile.astype(BF16)
    cg_part = cg_fin.at[c, z, own_rows]
    cga_c = line_copies(lambda d: cg_part, cg_part, cga_s, cga_r, lambda d: plane(d, 0))
    first_pass(11, 10)
    sa_x = exchange(lambda k: stats_a.at[0], lambda s: stats_a.at[s], sa_s, sa_r)
    first_pass(12, 11)
    label_rows(3, 4, 5)
    arrived(q1f, q2f, q3f, q4f)
    first_pass(13, 12)
    first_pass(14, 13)

    arrived(*cga_c)

    @functools.cache
    def cgz_copy(d):
        slot = cg_fin.at[c, z]
        return pltpu.make_async_remote_copy(
            slot, slot, cgz_s.at[d], cgz_r.at[d], device_id=column(d), device_id_type=MESH
        )

    for d in range(1, 8):
        cgz_copy(d).start()

    label_rows(6, 7, 8, 9)
    arrived(p5f, q5f, p6f, q6f)
    first_pass(15, 14)
    target = 10.0 * total(mem[...] * protos[...].astype(F32))
    head = lax.broadcasted_iota(jnp.int32, (4, ROWS), 0) == 0
    stats_b[0, 4:8, :] = jnp.where(head, target, coarse_loss)
    sb_x = exchange(lambda k: stats_b.at[0], lambda s: stats_b.at[s], sb_s, sb_r)

    @functools.cache
    def core_copy(t):
        return pltpu.make_async_remote_copy(
            z_out.at[t, 1 - c], core_in.at[t], co_s.at[t], co_r.at[t], device_id=(other, g), device_id_type=MESH
        )

    @functools.cache
    def z_copy(t, d):
        return pltpu.make_async_remote_copy(
            z_out.at[t, c, zof(d)], z_in.at[t, d], zo_s.at[t, d], zo_r.at[t, d],
            device_id=column(d), device_id_type=MESH,
        )

    @functools.cache
    def za_copy(t, d):
        slot = fin.at[t, c, z]
        return pltpu.make_async_remote_copy(
            slot, slot, za_s.at[t, d], za_r.at[t, d], device_id=column(d), device_id_type=MESH
        )

    @functools.cache
    def ca_copy(t):
        slot = fin.at[t, c]
        return pltpu.make_async_remote_copy(
            slot, slot, ca_s.at[t], ca_r.at[t], device_id=(other, g), device_id_type=MESH
        )

    def core_send(t, src):
        half = src[pl.ds(pl.multiple_of((1 - c) * 512, 512), 512), :].astype(BF16)
        z_out[t, 1 - c] = half.reshape(8, 64, D)
        core_copy(t).start()

    def core_merge(t, src):
        core_copy(t).wait_recv()
        half = src[pl.ds(pl.multiple_of(c * 512, 512), 512), :].reshape(8, 64, D)
        z_out[t, c] = (half + core_in[t].astype(F32)).astype(BF16)

        for d in range(1, 8):
            z_copy(t, d).start()

    def z_merge(t):
        for d in range(1, 8):
            z_copy(t, d).wait_recv()

        acc = z_out[t, c, z].astype(F32)
        for d in range(1, 8):
            acc = acc + z_in[t, d].astype(F32)
        fin[t, c, z] = acc.astype(BF16)

        for d in range(1, 8):
            za_copy(t, d).start()

    def z_gathered(t):
        for d in range(1, 8):
            za_copy(t, d).wait_recv()

        ca_copy(t).start()

    core_send(0, mem)

    last = None
    for rows in parts:
        last = add(last, dot(protos_t[:, rows], ebuf[15, rows, :]))
    obuf[15] = last
    label_rows(10, 11, 12, 13, 14, 15)
    core_merge(0, mem)

    arrived(*sa_x)
    arrived(*sb_x)

    def line(a, b, dx):
        away = (dx - a) % 4
        if away == 2:
            return stats_b[rel(a, b), 0:4, :]
        return stats_a[rel(a, b), SLOT[away] * 4 : SLOT[away] * 4 + 4, :]

    loss_rows = None
    for dx in range(4):
        lines = [line(a, b, dx) for a in range(4) for b in range(4)]
        peak = functools.reduce(jnp.maximum, lines)
        log_total = peak + jnp.log(functools.reduce(add, [jnp.exp(v - peak) for v in lines]))
        lt_a[dx] = log_total
        loss_rows = add(loss_rows, log_total)
    for k, (dx, dy) in enumerate(ORDER):
        wbuf[k : k + 1, :] = jnp.exp(mmax[k : k + 1, :] - lt_a[dx, pl.ds(ys[dy], 1), :])

    def row_terms(k):
        return 10.0 * (obuf[k] * wbuf[k : k + 1, :] - lbuf[k].astype(F32))

    rw_x = []
    for p in ROW_ORDER:
        k = ORDER.index(p)
        rout[k] = row_terms(k).astype(BF16)
        cp = pltpu.make_async_remote_copy(
            rout.at[k], rin.at[k], rw_s.at[k], rw_r.at[k], device_id=plane(*p), device_id_type=MESH
        )
        cp.start()
        rw_x.append((cp, k))
    for j, rows in enumerate(parts):
        acc = None
        for k, p in enumerate(ORDER):
            if j == 0:
                w_col = jnp.broadcast_to(wbuf[k : k + 1, :], (128, 256)).T
                for h in (slice(0, 128), slice(128, 256)):
                    us[k, :, h] = (gbuf[rel(*p), :, h].astype(F32) * w_col).astype(BF16)
            acc = add(acc, dot(ebuf[k, rows, :], us[k]))
        soft[rows, :] = acc

    core_send(1, soft)
    own_rt[...] = row_terms(0)
    sums = functools.reduce(add, [stats_b[k, 4:8, :] for k in range(G)])
    coarse_all = sums[1:2, 0:1]
    loss_core[0] = jnp.broadcast_to(total(loss_rows) - sums[0:1, 0:1], (8, 128))
    lcp = pltpu.make_async_remote_copy(
        loss_core.at[0], loss_core.at[1], ls_s.at[0], ls_r.at[0], device_id=(other, g), device_id_type=MESH
    )
    lcp.start()
    core_merge(1, soft)
    lcp.wait_recv()
    loss_z[0] = loss_core[0] + loss_core[1]

    @functools.cache
    def lz_copy(d):
        return pltpu.make_async_remote_copy(
            loss_z.at[0], loss_z.at[d], ls_s.at[d], ls_r.at[d], device_id=column(d), device_id_type=MESH
        )

    for d in range(1, 8):
        lz_copy(d).start()

    for rows in parts:
        cpart[rows, :] = cpart_t[:, rows].T
    for d in range(1, 8):
        cgz_copy(d).wait_recv()

    cg_mine = cg_fin.at[c]
    cgc = pltpu.make_async_remote_copy(
        cg_mine, cg_mine, cgz_s.at[0], cgz_r.at[0], device_id=(other, g), device_id_type=MESH
    )
    cgc.start()
    z_merge(0)
    cgc.wait_recv()
    o_cg[...] = cg_fin[...].reshape(KC, D).astype(F32)
    z_merge(1)
    z_gathered(0)
    ca_copy(0).wait_recv()
    for j, rows in enumerate(parts):
        members = fin[0, j // 2, (j % 2) * 4 : (j % 2) * 4 + 4].reshape(256, D).astype(F32)
        p32 = protos[rows, :].astype(F32)
        norm = jnp.sqrt(jnp.sum(p32 * p32, axis=1, keepdims=True) + 1e-06)
        length = lax.rsqrt(jnp.sum(members * members, axis=1, keepdims=True) + 1e-06)
        o_new[rows, :] = 0.5 * p32 + (0.5 * norm) * (members * length)
        cpart[rows, :] = cpart[rows, :] - 2.5 * members

    z_gathered(1)

    half = (G - 1) // 2
    acc = own_rt[...]
    for cp, k in rw_x[:half]:
        cp.wait_recv()
        acc = acc + rin[k].astype(F32)
    own_rt[...] = acc
    for cp in gathers + lab_x + cgx_c + cgy_c + cga_c + sa_x + sb_x:
        cp.wait_send()
    for d in range(1, 8):
        cgz_copy(d).wait_send()
        for t in range(2):
            z_copy(t, d).wait_send()
    core_copy(0).wait_send()
    core_copy(1).wait_send()
    lcp.wait_send()
    for d in range(1, 8):
        za_copy(0, d).wait_send()
    cgc.wait_send()
    ca_copy(0).wait_send()

    for d in range(1, 8):
        lz_copy(d).wait_recv()
    fine = functools.reduce(add, [loss_z[d] for d in range(8)])
    o_loss[...] = fine[0:1, 0:1] * (1.0 / (G * G * ROWS)) + coarse_all * (1.0 / (KL * G))

    ca_copy(1).wait_recv()
    for j, rows in enumerate(parts):
        part = fin[1, j // 2, (j % 2) * 4 : (j % 2) * 4 + 4].reshape(256, D).astype(F32)
        o_pg[rows, :] = cpart[rows, :] + 2.5 * part
    for d in range(1, 8):
        lz_copy(d).wait_send()
        za_copy(1, d).wait_send()
    ca_copy(1).wait_send()

    acc = own_rt[...]
    for cp, k in rw_x[half:]:
        cp.wait_recv()
        acc = acc + rin[k].astype(F32)
    row_grad = acc.T
    unit = unit_s[...]
    inv = inv_s[:, 0:1]
    o_emb[...] = inv * (row_grad - unit * jnp.sum(unit * row_grad, axis=1, keepdims=True))
    for cp, _ in rw_x:
        cp.wait_send()


def body(embeddings, fine_labels, prototypes, coarse_protos, coarse_labels):
    vmem = pl.BlockSpec(memory_space=pltpu.VMEM)
    sem = pltpu.SemaphoreType.DMA
    scratch = [
        pltpu.VMEM((G, ROWS, D), BF16),
        pltpu.VMEM((G, 1, ROWS), jnp.int32),
        pltpu.VMEM((ROWS, D), F32),
        pltpu.VMEM((ROWS, 128), F32),
        pltpu.VMEM((D, KL), BF16),
        pltpu.VMEM((D, KC), BF16),
        pltpu.VMEM((KL, ROWS), F32),
        pltpu.VMEM((KL, ROWS), F32),
        pltpu.VMEM((G, KL, ROWS), BF16),
        pltpu.VMEM((G, D, ROWS), F32),
        pltpu.VMEM((G, D, ROWS), BF16),
        pltpu.VMEM((G, ROWS, D), BF16),
        pltpu.VMEM((G, D, ROWS), BF16),
        pltpu.VMEM((G, D, ROWS), BF16),
        pltpu.VMEM((D, ROWS), F32),
        pltpu.VMEM((KL, D), F32),
        pltpu.VMEM((KL, D), F32),
        pltpu.VMEM((KC, D), F32),
        pltpu.VMEM((D, KL), F32),
        pltpu.VMEM((KL, D), F32),
        pltpu.VMEM((G, 16, ROWS), F32),
        pltpu.VMEM((G, 8, ROWS), F32),
        pltpu.VMEM((G, ROWS), F32),
        pltpu.VMEM((4, 4, ROWS), F32),
        pltpu.VMEM((G, ROWS), F32),
        pltpu.VMEM((4, 16, D), F32),
        pltpu.VMEM((4, 16, D), F32),
        pltpu.VMEM((2, 8, 64, D), BF16),
        pltpu.VMEM((2, 8, 64, D), BF16),
        pltpu.VMEM((2, 2, 8, 64, D), BF16),
        pltpu.VMEM((2, 8, 64, D), BF16),
        pltpu.VMEM((2, 2, 8, 64, D), BF16),
        pltpu.VMEM((2, 8, 128), F32),
        pltpu.VMEM((8, 8, 128), F32),
        sem((N_GATHER,)), sem((N_GATHER,)),
        sem((G,)), sem((G,)), sem((4,)), sem((4,)), sem((4,)), sem((4,)), sem((4,)), sem((4,)),
        sem((8,)), sem((8,)),
        sem((G,)), sem((G,)), sem((G,)), sem((G,)), sem((G,)), sem((G,)),
        sem((2,)), sem((2,)),
        sem((2, 8)), sem((2, 8)), sem((2, 8)), sem((2, 8)),
        sem((2,)), sem((2,)),
        sem((8,)), sem((8,)),
    ]
    outs = [
        pltpu.VMEM((ROWS, D), F32),
        pltpu.VMEM((KL, D), F32),
        pltpu.VMEM((KL, D), F32),
        pltpu.VMEM((KC, D), F32),
        jax.ShapeDtypeStruct((1, 1), F32),
    ]
    ge, gp, new, gc, loss = pl.pallas_call(
        kernel,
        out_shape=outs,
        in_specs=[vmem] * 5,
        out_specs=[vmem] * 5,
        scratch_shapes=scratch,
        compiler_params=pltpu.CompilerParams(
            collective_id=0, has_side_effects=True, vmem_limit_bytes=56 * 1024 * 1024
        ),
    )(embeddings, fine_labels.reshape(1, ROWS), prototypes, coarse_protos, coarse_labels.reshape(1, KC))
    return ge, gp, new, gc, loss.reshape(())


def solution(mesh):
    in_specs = (P(("rows", "group"), None), P(("rows", "group")), P("group", None), P(), P("group"))
    out_specs = (P(("rows", "group"), None), P("group", None), P("group", None), P(), P())
    return jax.shard_map(body, mesh=mesh, in_specs=in_specs, out_specs=out_specs, check_vma=False)
```
